32 devices in a mesh: dp: 8 (over z, x), tensor: 4 (over y, core).
Axes of the slice: x: 2, y: 2, z: 4, core: 2. Of those that a mesh axis runs over, the one named last changes fastest.
Arguments:
- patch_embeds: bfloat16 [32, 529, 768], P('dp'), may hold values from -6 to 6
- segment_ids: int32 [32, 529], P('dp'), may hold values from 0 to 3, never falling along the last dimension, each value on 1 to 264 neighbouring positions
- cotangent: bfloat16 [32, 529, 768], P('dp'), may hold values from -6 to 6
- ln1_gain: bfloat16 [768], P('dp'), may hold values from 0.5 to 1.5
- ln1_bias: bfloat16 [768], P('dp'), may hold values from -3 to 3
- w_query: bfloat16 [768, 768], P('dp', 'tensor'), may hold values from -0.21875 to 0.21875
- w_key: bfloat16 [768, 768], P('dp', 'tensor'), may hold values from -0.21875 to 0.21875
- w_value: bfloat16 [768, 768], P('dp', 'tensor'), may hold values from -0.21875 to 0.21875
- b_query: bfloat16 [12, 64], P('tensor', 'dp'), may hold values from -3 to 3
- b_value: bfloat16 [12, 64], P('tensor', 'dp'), may hold values from -3 to 3
- w_out: bfloat16 [768, 768], P('tensor', 'dp'), may hold values from -0.75 to 0.75
- b_out: bfloat16 [768], P('dp'), may hold values from -3 to 3
- ln2_gain: bfloat16 [768], P('dp'), may hold values from 0.5 to 1.5
- ln2_bias: bfloat16 [768], P('dp'), may hold values from -3 to 3
- w_fc1: bfloat16 [768, 3072], P('dp', 'tensor'), may hold values from -0.21875 to 0.21875
- b_fc1: bfloat16 [48, 64], P('tensor', 'dp'), may hold values from -3 to 3
- w_fc2: bfloat16 [3072, 768], P('tensor', 'dp'), may hold values from -0.109375 to 0.109375
- b_fc2: bfloat16 [768], P('dp'), may hold values from -3 to 3
Outputs:
- block_out: bfloat16 [32, 529, 768], P('dp')
- grad_patches: bfloat16 [32, 529, 768], P('dp')
- g_ln1_gain: float32 [768], P('dp')
- g_ln1_bias: float32 [768], P('dp')
- g_w_query: float32 [768, 768], P('dp', 'tensor')
- g_w_key: float32 [768, 768], P('dp', 'tensor')
- g_w_value: float32 [768, 768], P('dp', 'tensor')
- g_b_query: float32 [12, 64], P('tensor', 'dp')
- g_b_value: float32 [12, 64], P('tensor', 'dp')
- g_w_out: float32 [768, 768], P('tensor', 'dp')
- g_b_out: float32 [768], P('dp')
- g_ln2_gain: float32 [768], P('dp')
- g_ln2_bias: float32 [768], P('dp')
- g_w_fc1: float32 [768, 3072], P('dp', 'tensor')
- g_b_fc1: float32 [48, 64], P('tensor', 'dp')
- g_w_fc2: float32 [3072, 768], P('tensor', 'dp')
- g_b_fc2: float32 [768], P('dp')
The draws below stay inside these ranges and needn't reach their ends.
Inputs may be any that keep to these rules, and one draw needn't show every extreme that they name: `segment_ids`: along each strip the ids never fall; each of the 4 documents has 1 to 529 // 2 patches, and one document of each strip has exactly that many.
All inputs are finite; a program needn't handle non-finite values.
Results may differ from the reference program's by a relative error of at most 0.022.
Values may be sent and summed in bfloat16 or wider, within the bound.
No kernel may reach another device: no remote copies, remote signals or barrier semaphores. Data moves between devices by JAX's collectives and lax.ppermute only.
A program may use at most 192 MiB of HBM per device.

```python
import math
import jax
import jax.numpy as jnp
import numpy as np
from jax import lax

HD = 64
HEADS = 12
D = 768
FF = 3072
SEG = 529
DOCS = 4
STRIPS = 32


def steps_of(own_key, dims, cuts, low, largest):
    gain, own = 1.0, jax.random.fold_in(own_key, 6)
    for dim, blocks in cuts:
        heights = jnp.exp(jax.random.uniform(jax.random.fold_in(own, dim), (blocks,), jnp.float32, low / len(cuts), largest / len(cuts)))
        gain = gain * jnp.repeat(heights, dims[dim] // blocks).reshape([-1 if axis == dim else 1 for axis in range(len(dims))])
    return gain


def length_profile(amount, total, most, slope):
    weights = [(1 << 20) // math.isqrt(rank ** slope) + 1 for rank in range(2, amount + 1)]
    surplus, given = total - most - (amount - 1), [1] * (amount - 1)
    while surplus > 0:
        movable = [i for i in range(amount - 1) if given[i] < most]
        pool, left = sum([weights[i] for i in movable]), surplus
        for i in movable:
            addition = min(most - given[i], max(1, left * weights[i] // pool), surplus)
            given[i] = given[i] + addition
            surplus = surplus - addition
    return np.array([most] + given)


def ragged_sizes(own_key, amount, total, limit, slope):
    if amount == 2:
        one = jax.random.randint(own_key, (), max(1, total - limit), min(limit, total - 1) + 1)
        return jnp.stack([one, total - one])
    lengths = jnp.asarray(length_profile(amount, total, limit, slope), jnp.int32)
    pairs = (amount - 1) // 2
    source_of, receiver = lengths[1:1 + 2 * pairs:2], lengths[2:2 + 2 * pairs:2]
    room = jnp.minimum(source_of - 1, limit - receiver)
    moved = jax.random.randint(jax.random.fold_in(own_key, 1), (pairs,), 0, 1 << 20) % (room + 1)
    lengths = lengths.at[1:1 + 2 * pairs:2].set(source_of - moved).at[2:2 + 2 * pairs:2].set(receiver + moved)
    return lengths[jax.random.permutation(jax.random.fold_in(own_key, 2), amount)]


def normal_values(key, dims, scale, limit, cuts=(), kind=jnp.bfloat16):
    array = scale * jax.random.normal(key, dims, jnp.float32)
    if cuts:
        array = array * steps_of(key, dims, cuts, -0.22, 0.18)
    return jnp.clip(array, -limit, limit).astype(kind)


def setup_inputs(seed: int = 0) -> dict:
    streams_of = jax.random.split(jax.random.key(seed), 19)
    return {
        "patch_embeds": normal_values(streams_of[0], (STRIPS, SEG, D), 1.0, 6.0, ((0, 8),)),
        "segment_ids": jax.vmap(lambda own: jnp.searchsorted(jnp.cumsum(ragged_sizes(own, DOCS, SEG, SEG // 2, 2)), jnp.arange(SEG), side="right"))(jax.random.split(streams_of[1], STRIPS)).reshape((STRIPS, SEG)).astype(jnp.int32),
        "cotangent": normal_values(streams_of[2], (STRIPS, SEG, D), 1.0, 6.0, ((0, 8),)),
        "ln1_gain": jnp.clip(1.0 + 0.1 * jax.random.normal(streams_of[3], (D,), jnp.float32), 0.5, 1.5).astype(jnp.bfloat16),
        "ln1_bias": normal_values(streams_of[4], (D,), 0.5, 3.0, ((0, 8),)),
        "w_query": normal_values(streams_of[5], (D, D), D ** -0.5, 0.21875, ((0, 8), (1, 4))),
        "w_key": normal_values(streams_of[6], (D, D), D ** -0.5, 0.21875, ((0, 8), (1, 4))),
        "w_value": normal_values(streams_of[7], (D, D), D ** -0.5, 0.21875, ((0, 8), (1, 4))),
        "b_query": normal_values(streams_of[8], (HEADS, HD), 0.5, 3.0, ((0, 4), (1, 8))),
        "b_value": normal_values(streams_of[9], (HEADS, HD), 0.5, 3.0, ((0, 4), (1, 8))),
        "w_out": normal_values(streams_of[10], (D, D), HD ** -0.5, 0.75, ((0, 4), (1, 8))),
        "b_out": normal_values(streams_of[11], (D,), 0.5, 3.0, ((0, 8),)),
        "ln2_gain": jnp.clip(1.0 + 0.1 * jax.random.normal(streams_of[12], (D,), jnp.float32), 0.5, 1.5).astype(jnp.bfloat16),
        "ln2_bias": normal_values(streams_of[13], (D,), 0.5, 3.0, ((0, 8),)),
        "w_fc1": normal_values(streams_of[14], (D, FF), D ** -0.5, 0.21875, ((0, 8), (1, 4))),
        "b_fc1": normal_values(streams_of[15], (FF // HD, HD), 0.5, 3.0, ((0, 4), (1, 8))),
        "w_fc2": normal_values(streams_of[16], (FF, D), FF ** -0.5, 0.109375, ((0, 4), (1, 8))),
        "b_fc2": normal_values(streams_of[17], (D,), 0.5, 3.0, ((0, 8),)),
    }


@jax.custom_vjp
def low(v):
    return lax.optimization_barrier(v.astype(jnp.bfloat16)).astype(jnp.float32)

@jax.custom_vjp
def low_back(v):
    return v

def low_keep(v):
    return (low(v), None)

def low_pass(kept, grad):
    return (grad,)

def back_keep(v):
    return (v, None)

def back_low(kept, grad):
    return (low(grad),)
low.defvjp(low_keep, low_pass)
low_back.defvjp(back_keep, back_low)
eps_norm = 1e-06

def matmul_high(left, right):
    return jnp.dot(left, right, precision=lax.Precision.HIGHEST, preferred_element_type=jnp.float32)

def rounded(values):
    return low(low_back(values))

def layer_norm(values, ln_gain, ln_shift):
    centre = values - lax.optimization_barrier(jnp.mean(values, axis=-1, keepdims=True))
    spread = lax.optimization_barrier(jnp.mean(centre * centre, axis=-1, keepdims=True))
    return centre * lax.rsqrt(spread + eps_norm) * ln_gain + ln_shift

def attend(pieces):
    query, key_part, value_part, seg_part = pieces
    raw_scores = jnp.einsum('qhd,khd->hqk', query, key_part, precision=lax.Precision.HIGHEST) * HD ** (-0.5)
    same_doc = seg_part[:, None] == seg_part[None, :]
    masked = low_back(jnp.where(same_doc[None], raw_scores, -1e+30))
    weights = low(jax.nn.softmax(masked, axis=-1))
    return jnp.einsum('hqk,khd->qhd', weights, value_part, precision=lax.Precision.HIGHEST)

def reference(patch_embeds, segment_ids, cotangent, ln1_gain, ln1_bias, w_query, w_key, w_value, b_query, b_value, w_out, b_out, ln2_gain, ln2_bias, w_fc1, b_fc1, w_fc2, b_fc2):
    params = tuple((p.astype(jnp.float32) for p in (ln1_gain, ln1_bias, w_query, w_key, w_value, b_query, b_value, w_out, b_out, ln2_gain, ln2_bias, w_fc1, b_fc1, w_fc2, b_fc2)))
    inputs = patch_embeds.astype(jnp.float32)

    def forward(x_in, gain_one, shift_one, wq_f, wk_f, wv_f, bq_f, bv_f, wo_f, bo_f, gain_two, shift_two, w1_f, b1_f, w2_f, b2_f):
        flat_rows = x_in.reshape(-1, D)
        normed_one = low(layer_norm(flat_rows, gain_one, shift_one))
        query = rounded(matmul_high(normed_one, wq_f) + bq_f.reshape(-1))
        keys_all = rounded(matmul_high(normed_one, wk_f))
        values_all = rounded(matmul_high(normed_one, wv_f) + bv_f.reshape(-1))
        split = (-1, SEG, HEADS, HD)
        attended = lax.map(jax.checkpoint(attend), (query.reshape(split), keys_all.reshape(split), values_all.reshape(split), segment_ids))
        attended = rounded(attended.reshape(-1, D))
        middle = flat_rows + low_back(matmul_high(attended, wo_f)) + bo_f
        normed_two = low(layer_norm(middle, gain_two, shift_two))
        hidden_pre = low_back(matmul_high(normed_two, w1_f) + b1_f.reshape(-1))
        hidden = low(jax.nn.gelu(hidden_pre, approximate=False))
        output = middle + matmul_high(hidden, w2_f) + b2_f
        return output.reshape(x_in.shape)
    output, pull = jax.vjp(forward, inputs, *params)
    grads = pull(cotangent.astype(jnp.float32))
    return (output.astype(jnp.bfloat16), grads[0].astype(jnp.bfloat16), grads[1], grads[2], grads[3], grads[4], grads[5], grads[6], grads[7], grads[8], grads[9], grads[10], grads[11], grads[12], grads[13], grads[14], grads[15])
```

```python
import functools

import jax
import jax.numpy as jnp
from jax import lax
from jax.experimental import pallas as pl
from jax.experimental.pallas import tpu as pltpu
from jax.sharding import PartitionSpec as P

HD = 64
EPS = 1e-06
BIG = 2.0**100
BF = jnp.bfloat16
F32 = jnp.float32
VEC = 8
COST = 1
VMEM_LIMIT = 48 * 1024 * 1024


def nn(a, b):
    return lax.dot_general(a, b, (((1,), (0,)), ((), ())), preferred_element_type=F32)


def nt(a, b):
    return lax.dot_general(a, b, (((1,), (1,)), ((), ())), preferred_element_type=F32)


def tn(a, b):
    return lax.dot_general(a, b, (((0,), (0,)), ((), ())), preferred_element_type=F32)


def norm_parts(v):
    c = v - jnp.mean(v, axis=-1, keepdims=True)
    rstd = lax.rsqrt(jnp.mean(c * c, axis=-1, keepdims=True) + EPS)
    return c * rstd, rstd


def norm_back(grad, gain, xhat, rstd):
    scaled = grad * gain
    m1 = jnp.mean(scaled, axis=-1, keepdims=True)
    m2 = jnp.mean(scaled * xhat, axis=-1, keepdims=True)
    return rstd * (scaled - m1 - xhat * m2)


def colsum(v):
    return jnp.sum(v, axis=0, keepdims=True)


def take_block(step, a_ref, b_ref, scr):
    @pl.when(step == 0)
    def _():
        scr[...] = a_ref[...]

    @pl.when(step == 1)
    def _():
        scr[...] = b_ref[...]


def attend_block(rows, heads, n1, scr, seg_ref, vec_ref, qe_ref, ke_ref, ve_ref, e_ref, att_ref, inv_ref):
    width = scr.shape[2]
    hw = heads * HD
    w = scr[:, :rows, :].reshape(width, width)
    vec = jnp.sum(scr[:, rows:, :].astype(F32), axis=0)
    vec_ref[0] = vec
    length = n1.shape[0]
    proj = nn(n1, w[:, : 3 * hw])
    bq = vec[7:8, :hw]
    bv = vec[7:8, hw : 2 * hw]
    q = ((proj[:, :hw] + bq).astype(BF).astype(F32) * (HD**-0.5)).astype(BF)
    k = proj[:, hw : 2 * hw].astype(BF)
    v = (proj[:, 2 * hw :] + bv).astype(BF)
    lane = lax.broadcasted_iota(jnp.int32, (length, HD), 1)
    hot = jnp.where(lane == seg_ref[...], 1.0, 0.0)
    ext_k = jnp.where(lane < 4, hot, 0.0).astype(BF)
    ext_q = jnp.where(lane < 4, (hot - 1.0) * BIG, 0.0).astype(BF)
    ext_v = jnp.where(lane < 2, 1.0, 0.0).astype(BF)
    atts = [jnp.zeros((length, HD), BF)]
    invs = [jnp.zeros((length, HD), F32)]
    for h in range(heads):
        cut = slice(h * HD, (h + 1) * HD)
        qe = jnp.concatenate([q[:, cut], ext_q], axis=1)
        ke = jnp.concatenate([k[:, cut], ext_k], axis=1)
        ve = jnp.concatenate([v[:, cut], ext_v], axis=1)
        qe_ref[0, h] = qe
        ke_ref[0, h] = ke
        ve_ref[0, h] = ve
        s = nt(ke, qe)
        e = jnp.exp(s - jnp.max(s, axis=0, keepdims=True)).astype(BF)
        e_ref[0, h] = e
        o = tn(e, ve)
        inv = 1.0 / o[:, HD : HD + 1]
        atts.append((o[:, :HD] * inv).astype(BF))
        invs.append(jnp.broadcast_to(inv, (length, HD)))
    att = jnp.concatenate(atts, axis=1)
    att_ref[0] = att
    inv_ref[0] = jnp.concatenate(invs, axis=1)
    return nt(att, w[:, 3 * hw - HD :])


def attn_fwd_first(rows, heads, x_ref, seg_ref, a_ref, b_ref, n1_ref, part_ref, vec_ref, qe_ref, ke_ref, ve_ref, e_ref, att_ref, inv_ref, scr):
    step = pl.program_id(0)
    take_block(step, a_ref, b_ref, scr)

    @pl.when(step == 0)
    def _():
        vec = jnp.sum(a_ref[:, rows:, :].astype(F32), axis=0)
        xhat, _ = norm_parts(x_ref[...].astype(F32))
        n1_ref[...] = (xhat * vec[0:1] + vec[1:2]).astype(BF)
        part_ref[...] = jnp.zeros_like(part_ref)

    part_ref[...] += attend_block(rows, heads, n1_ref[...], scr, seg_ref, vec_ref, qe_ref, ke_ref, ve_ref, e_ref, att_ref, inv_ref)


def attn_fwd_second(rows, heads, x_ref, n1_ref, part_ref, dvec_ref, seg_ref, a_ref, b_ref, k0, k1, k2, k3, k4, k5, k6, mid_ref, n2_ref, vec_ref, qe_ref, ke_ref, ve_ref, e_ref, att_ref, inv_ref, scr):
    step = pl.program_id(0)
    take_block(step, a_ref, b_ref, scr)
    more = attend_block(rows, heads, n1_ref[...], scr, seg_ref, vec_ref, qe_ref, ke_ref, ve_ref, e_ref, att_ref, inv_ref)

    @pl.when(step == 0)
    def _():
        mid_ref[...] = x_ref[...].astype(F32) + dvec_ref[0, 4:5] + part_ref[...] + more

    @pl.when(step == 1)
    def _():
        middle = mid_ref[...] + more
        mid_ref[...] = middle
        xhat, _ = norm_parts(middle)
        n2_ref[...] = (xhat * dvec_ref[0, 2:3] + dvec_ref[0, 3:4]).astype(BF)


def gelu_both(x):
    z = jnp.abs(x) * (0.5**0.5)
    t = 1.0 / (1.0 + 0.3275911 * z)
    gauss = jnp.exp(x * x * -0.5)
    poly = t * (0.254829592 + t * (-0.284496736 + t * (1.421413741 + t * (-1.453152027 + t * 1.061405429))))
    tail = 0.5 * poly * gauss
    cdf = jnp.where(x < 0, tail, 1.0 - tail)
    return x * cdf, cdf + x * gauss * 0.3989422804014327


def mlp_block(rows, n2, dy, w_ref, b1_row, g_ref, gb_ref):
    width = w_ref.shape[3]
    w1 = w_ref[:, 0, :rows, :].reshape(width, width)
    w2t = w_ref[:, 0, rows:, :].reshape(width, width)
    out = None
    back = None
    chunk = 256
    for c in range(width // chunk):
        cut = slice(c * chunk, (c + 1) * chunk)
        w1c = w1[:, cut]
        w2c = w2t[:, cut]
        pre = nn(n2, w1c) + b1_row[:, cut]
        hid, slope = gelu_both(pre)
        hid = hid.astype(BF)
        gpre = (nn(dy, w2c) * slope).astype(BF)
        gb_ref[0, 0:1, cut] = colsum(gpre.astype(F32))
        g_ref[0, 0, :, cut] = tn(n2, gpre).astype(BF)
        g_ref[0, 1, :, cut] = tn(dy, hid).astype(BF)
        more_out = nt(hid, w2c)
        more_back = nt(gpre, w1c)
        out = more_out if out is None else out + more_out
        back = more_back if back is None else back + more_back
    return out, back


def mlp_first(rows, ids_ref, n2_ref, dy_ref, w_ref, b1_ref, out_ref, back_ref, g_ref, gb_ref):
    out, back = mlp_block(rows, n2_ref[...], dy_ref[...], w_ref, b1_ref[0, 6:7], g_ref, gb_ref)

    @pl.when(pl.program_id(0) == 0)
    def _():
        out_ref[...] = out
        back_ref[...] = back

    @pl.when(pl.program_id(0) == 1)
    def _():
        out_ref[...] += out
        back_ref[...] += back


def mlp_second(rows, ids_ref, n2_ref, dy_ref, w_ref, b1_ref, out0_ref, back0_ref, mid_ref, dvec_ref, y_ref, gm_ref, gml_ref, vg_ref, g_ref, gb_ref, out_ref, back_ref):
    out, back = mlp_block(rows, n2_ref[...], dy_ref[...], w_ref, b1_ref[0, 6:7], g_ref, gb_ref)

    @pl.when(pl.program_id(0) == 0)
    def _():
        out_ref[...] = out0_ref[...] + out
        back_ref[...] = back0_ref[...] + back

    @pl.when(pl.program_id(0) == 1)
    def _():
        middle = mid_ref[...]
        dy = dy_ref[...].astype(F32)
        y_ref[...] = (middle + out_ref[...] + out + dvec_ref[0, 5:6]).astype(BF)
        grad = back_ref[...] + back
        xhat, rstd = norm_parts(middle)
        gm = dy + norm_back(grad, dvec_ref[0, 2:3], xhat, rstd)
        gm_ref[...] = gm
        gml_ref[...] = gm.astype(BF)
        vg_ref[0:1] = colsum(grad * xhat)
        vg_ref[1:2] = colsum(grad)
        vg_ref[2:3] = colsum(gm)
        vg_ref[3:4] = colsum(dy)


def attend_back(rows, heads, n1, gml, scr, qe_ref, ke_ref, ve_ref, e_ref, att_ref, inv_ref, g_ref, gb_ref):
    width = scr.shape[2]
    hw = heads * HD
    half = width // 2
    w = scr[:, :rows, :].reshape(width, width)
    length = n1.shape[0]
    att = att_ref[0]
    ga = nn(gml, w[:, 3 * hw - HD :]).astype(BF).astype(F32) * inv_ref[0]
    do = ga.astype(BF)
    prod = do.astype(F32) * att.astype(F32)
    lane = lax.broadcasted_iota(jnp.int32, (length, HD), 1)
    dqs, dks, dvs = [], [], []
    for h in range(heads):
        cut = slice((h + 1) * HD, (h + 2) * HD)
        delta = -jnp.sum(prod[:, cut], axis=1, keepdims=True)
        high = delta.astype(BF).astype(F32)
        ext = jnp.where(lane == 0, high, jnp.where(lane == 1, delta - high, 0.0)).astype(BF)
        doe = jnp.concatenate([do[:, cut], ext], axis=1)
        e = e_ref[0, h]
        dp = nt(ve_ref[0, h], doe)
        ds = (e.astype(F32) * dp).astype(BF)
        dqs.append((tn(ds, ke_ref[0, h])[:, :HD] * (HD**-0.5)).astype(BF))
        dks.append(nn(ds, qe_ref[0, h][:, :HD]).astype(BF))
        dvs.append(nn(e, do[:, cut]).astype(BF))
    dqkv = jnp.concatenate(dqs + dks + dvs, axis=1)
    last = jnp.concatenate([dvs[-1], jnp.zeros((length, hw), BF)], axis=1)
    split = 3 * hw - HD
    ga_first = tn(n1, dqkv[:, :half]).astype(BF)
    g_ref[0, 0] = ga_first
    g_ref[0, 1, :, : split - half] = tn(n1, dqkv[:, half:split]).astype(BF)
    g_ref[0, 1, :, split - half :] = (tn(n1, last) + tn(gml, att)).astype(BF)
    gb_ref[0, 0:1] = colsum(dqkv.astype(F32))
    return nt(dqkv, w[:, : 3 * hw])


def attn_back_first(rows, heads, n1_ref, gml_ref, a_ref, b_ref, qe_ref, ke_ref, ve_ref, e_ref, att_ref, inv_ref, back_ref, g_ref, gb_ref, scr):
    step = pl.program_id(0)
    take_block(step, a_ref, b_ref, scr)
    back = attend_back(rows, heads, n1_ref[...], gml_ref[...], scr, qe_ref, ke_ref, ve_ref, e_ref, att_ref, inv_ref, g_ref, gb_ref)

    @pl.when(step == 0)
    def _():
        back_ref[...] = back

    @pl.when(step == 1)
    def _():
        back_ref[...] += back


def attn_back_second(rows, heads, n1_ref, gml_ref, a_ref, b_ref, qe_ref, ke_ref, ve_ref, e_ref, att_ref, inv_ref, x_ref, gm_ref, back0_ref, dvec_ref, gx_ref, vg_ref, g_ref, gb_ref, scr, back_ref):
    step = pl.program_id(0)
    take_block(step, a_ref, b_ref, scr)
    back = attend_back(rows, heads, n1_ref[...], gml_ref[...], scr, qe_ref, ke_ref, ve_ref, e_ref, att_ref, inv_ref, g_ref, gb_ref)

    @pl.when(step == 0)
    def _():
        back_ref[...] = back0_ref[...] + back

    @pl.when(step == 1)
    def _():
        grad = back_ref[...] + back
        xhat, rstd = norm_parts(x_ref[...].astype(F32))
        gx_ref[...] = (gm_ref[...] + norm_back(grad, dvec_ref[0, 0:1], xhat, rstd)).astype(BF)
        vg_ref[0:1] = colsum(grad * xhat)
        vg_ref[1:2] = colsum(grad)


def whole_block(shape):
    return pl.BlockSpec(shape, lambda *_: (0,) * len(shape))


def step_block(shape, first, stride):
    rest = (0,) * (len(shape) - 1)
    return pl.BlockSpec((1,) + shape[1:], lambda i, *_: (first + stride * i,) + rest)


def call(kernel, args, in_kinds, outs, out_kinds, scratch, flops, order=(0, 1), out_order=None, aliases=None):
    def make(order):
        return {
            "w": whole_block,
            "s": lambda shape: step_block(shape, order[0], order[1] - order[0]),
            "a": lambda shape: pl.BlockSpec(memory_space=pl.ANY),
        }

    ins = make(order)
    out_specs = make(out_order or order)
    moved = sum(a.size * a.dtype.itemsize for a in args) + sum(o.size * o.dtype.itemsize for o in outs)
    return pl.pallas_call(
        kernel,
        grid=(2,),
        in_specs=[ins[kind](a.shape) for kind, a in zip(in_kinds, args)],
        out_specs=[out_specs[kind](o.shape) for kind, o in zip(out_kinds, outs)],
        out_shape=outs,
        scratch_shapes=scratch,
        input_output_aliases=aliases or {},
        compiler_params=pltpu.CompilerParams(vmem_limit_bytes=VMEM_LIMIT),
        cost_estimate=pl.CostEstimate(flops=flops * COST, bytes_accessed=moved, transcendentals=0),
    )(*args)


def after(value, *others):
    return lax.optimization_barrier((value,) + others)[0]


def sds(shape, dtype):
    return jax.ShapeDtypeStruct(shape, dtype)


def make_body(mesh):
    nd = mesh.shape["dp"]
    nt_ax = mesh.shape["tensor"]
    bits = nd.bit_length() - 1

    def xch(v, axis, bit):
        n = mesh.shape[axis]
        return lax.ppermute(v, axis, [(i, i ^ (1 << bit)) for i in range(n)])

    def bit_of(axis, bit):
        return ((lax.axis_index(axis) >> bit) & 1) == 1

    def body(
        patch_embeds,
        segment_ids,
        cotangent,
        ln1_gain,
        ln1_bias,
        w_query,
        w_key,
        w_value,
        b_query,
        b_value,
        w_out,
        b_out,
        ln2_gain,
        ln2_bias,
        w_fc1,
        b_fc1,
        w_fc2,
        b_fc2,
    ):
        strips, length, width = patch_embeds.shape
        assert strips == nt_ax == 4
        rows = width // nd
        heads = b_query.shape[0]
        hw = heads * HD
        per = HD // nd
        me_t = lax.axis_index("tensor")
        me_d = lax.axis_index("dp")
        x = lax.dynamic_index_in_dim(patch_embeds, me_t, 0, keepdims=False)
        dy = lax.dynamic_index_in_dim(cotangent, me_t, 0, keepdims=False)
        seg = lax.dynamic_index_in_dim(segment_ids, me_t, 0, keepdims=False)[:, None]

        def place(v, total, at):
            wide = jnp.zeros(v.shape[:-1] + (total,), BF)
            return lax.dynamic_update_slice_in_dim(wide, v, at, v.ndim - 1)

        six = jnp.stack([ln1_gain, ln1_bias, ln2_gain, ln2_bias, b_out, b_fc2])
        six = place(six, width, me_d * rows)
        heads_vec = place(jnp.concatenate([b_query, b_value, b_fc1]), HD, me_d * per)
        vec = jnp.concatenate(
            [
                six,
                heads_vec[2 * heads :].reshape(1, width),
                jnp.pad(heads_vec[: 2 * heads].reshape(1, 2 * hw), ((0, 0), (0, width - 2 * hw))),
            ]
        )
        share1 = jnp.concatenate(
            [jnp.concatenate([w_query, w_key, w_value, w_out.T], axis=1), vec]
        )
        share2 = jnp.concatenate([w_fc1, w_fc2.T])
        fc = lax.all_gather(share2, ("dp", "tensor"), axis=0, tiled=False)
        fc = fc.reshape(nd, nt_ax, 2 * rows, width)

        def spread(v, bit, axis):
            r = xch(v, "dp", bit)
            high = bit_of("dp", bit)
            return jnp.stack([jnp.where(high, r, v), jnp.where(high, v, r)], axis=axis)

        quarter = share1[None]
        for bit in reversed(range(1, bits)):
            quarter = spread(quarter, bit, 1).reshape(-1, rows + VEC, width)
        far = xch(quarter, "tensor", 1)
        v0 = spread(quarter, 0, 1).reshape(nd, rows + VEC, width)
        v1 = xch(v0, "tensor", 0)

        row32 = sds((length, width), F32)
        row16 = sds((length, width), BF)
        head = sds((4, heads, length, 2 * HD), BF)
        kept = [
            sds((4, VEC, width), F32),
            head,
            head,
            head,
            sds((4, heads, length, length), BF),
            sds((4, length, width - 3 * hw + HD), BF),
            sds((4, length, width - 3 * hw + HD), F32),
        ]
        block_scr = pltpu.VMEM((nd, rows + VEC, width), BF)
        big = 2 * length * width * width
        att_flops = 2 * big + 4 * heads * length * length * 4 * HD
        n1, part, *kept_a = call(
            functools.partial(attn_fwd_first, rows, heads),
            [x, seg, v0, v1],
            "wwww",
            [row16, row32] + kept,
            "wwsssssss",
            [block_scr],
            att_flops,
        )
        dvec = kept_a[0]
        v2 = spread(far, 0, 1).reshape(nd, rows + VEC, width)
        v3 = xch(v2, "tensor", 0)
        middle, n2, *kept_b = call(
            functools.partial(attn_fwd_second, rows, heads),
            [x, n1, part, dvec, seg, v2, v3] + kept_a,
            "wwwwwww" + "a" * 7,
            [row32, row16] + kept,
            "wwsssssss",
            [block_scr],
            att_flops,
            out_order=(2, 3),
            aliases={7 + i: 2 + i for i in range(7)},
        )
        vec_all = kept_b[0]

        w_block = (nd, 1, 2 * rows, width)

        def mlp_call(kernel, first, more, outs, scratch):
            ids = jnp.stack([me_t ^ first, me_t ^ (first - 2)])
            args = [n2, dy, fc, vec_all] + more
            specs = [
                whole_block(n2.shape),
                whole_block(dy.shape),
                pl.BlockSpec(w_block, lambda i, ids: (0, ids[i], 0, 0)),
                step_block(vec_all.shape, first, -2),
            ] + [whole_block(m.shape) for m in more]
            g_outs = [sds((2, 2, width, width), BF), sds((2, 1, width), F32)]
            return pl.pallas_call(
                kernel,
                grid_spec=pltpu.PrefetchScalarGridSpec(
                    num_scalar_prefetch=1,
                    grid=(2,),
                    in_specs=specs,
                    out_specs=[whole_block(o.shape) for o in outs] + [step_block(o.shape, 0, 1) for o in g_outs],
                    scratch_shapes=scratch,
                ),
                out_shape=outs + g_outs,
                compiler_params=pltpu.CompilerParams(vmem_limit_bytes=VMEM_LIMIT),
                cost_estimate=pl.CostEstimate(flops=12 * big * COST, bytes_accessed=20 * 2**20, transcendentals=0),
            )(ids, *args)

        out_b, back_b, g_fc_b, gb1_b = mlp_call(functools.partial(mlp_first, rows), 3, [], [row32, row32], [])
        got_fc = xch(g_fc_b, "tensor", 0)
        y, gm, gml, vg2, g_fc_a, gb1_a = mlp_call(
            functools.partial(mlp_second, rows),
            2,
            [out_b, back_b, middle, dvec],
            [row16, row32, row16, sds((4, width), F32)],
            [pltpu.VMEM((length, width), F32)] * 2,
        )
        block_out = lax.all_gather(y, "tensor", axis=0, tiled=False)

        def add(a, b):
            return (a.astype(F32) + b.astype(F32)).astype(BF)

        def parts(v, bit):
            high = bit_of("dp", bit)
            v = v.reshape(v.shape[:-3] + (v.shape[-3] // 2, 2) + v.shape[-2:])
            lo, hi = v[..., 0, :, :], v[..., 1, :, :]
            return jnp.where(high, hi, lo), jnp.where(high, lo, hi)

        def cut(v):
            return v.reshape(v.shape[:-2] + (nd, rows, v.shape[-1]))

        fc_sum = add(g_fc_a, got_fc)
        fc_keep1, fc_send1 = parts(cut(fc_sum[:, 1]), 0)
        fc_far0 = xch(cut(fc_sum[0, 0]), "tensor", 1)
        fc_near1 = xch(fc_send1, "dp", 0)
        gml = after(gml, fc_sum, fc_send1)

        g_in = sds((2, 2, width, width // 2), BF)
        gb_in = sds((2, 1, 3 * hw), F32)
        back_flops = 4 * big + 10 * heads * length * length * 4 * HD
        saved = kept_b[1:]
        back1, g_in_b, gbh_b = call(
            functools.partial(attn_back_first, rows, heads),
            [n1, gml, v3, v1] + saved,
            "wwww" + "ssssss",
            [row32, g_in, gb_in],
            "wss",
            [block_scr],
            back_flops,
            order=(3, 1),
            out_order=(0, 1),
        )
        got_in = xch(g_in_b, "tensor", 0)
        gx, vg1, g_in_a, gbh_a = call(
            functools.partial(attn_back_second, rows, heads),
            [n1, gml, v2, v0] + saved + [x, gm, back1, dvec],
            "wwww" + "ssssss" + "wwww",
            [row16, sds((2, width), F32), g_in, gb_in],
            "wwss",
            [block_scr, pltpu.VMEM((length, width), F32)],
            back_flops,
            order=(2, 0),
            out_order=(0, 1),
        )

        order = me_t ^ jnp.arange(4)
        hidden_rows = jnp.stack([gb1_a[1, 0], gb1_b[1, 0], gb1_a[0, 0], gb1_b[0, 0]])
        head_rows = jnp.stack([gbh_a[1, 0], gbh_b[1, 0], gbh_a[0, 0], gbh_b[0, 0]])
        head_rows = jnp.pad(head_rows, ((0, 0), (0, width - 3 * hw)))
        lanes = jnp.concatenate([hidden_rows, head_rows], axis=1)[order].reshape(8, width)
        small = jnp.concatenate([vg1, vg2, jnp.zeros((2, width), F32), lanes]).astype(BF)
        small = add(small, xch(small, "tensor", 0))
        half = width // 2
        n_small = 2 * small.shape[0]

        def xch_with(v, small, axis, bit):
            flat = jnp.concatenate([v.reshape(-1, half), small.reshape(n_small, half)])
            got = xch(flat, axis, bit)
            return got[:-n_small].reshape(v.shape), add(small, got[-n_small:].reshape(small.shape))

        in_sum = add(g_in_a, got_in)
        in_keep1, in_send1 = parts(cut(in_sum[:, 1]), 0)
        in_far0, small = xch_with(cut(in_sum[0, 0]), small, "tensor", 1)
        in_near1 = xch(in_send1, "dp", 0)

        fc_keep0, fc_send0 = parts(add(cut(fc_sum[1, 0]), fc_far0), 0)
        fc_near0 = xch(fc_send0, "dp", 0)
        fc_half1 = add(fc_keep1, fc_near1)
        fc_far1 = xch(fc_half1[0], "tensor", 1)
        g_fc = jnp.stack([add(fc_keep0, fc_near0), add(fc_half1[1], fc_far1)])
        for bit in range(1, bits):
            keep, send = parts(g_fc, bit)
            g_fc = add(keep, xch(send, "dp", bit))

        gy = xch(gx, "tensor", 1)
        pair = jnp.stack([gx, gy])
        other = xch(pair, "tensor", 0)

        in_keep0, in_send0 = parts(add(cut(in_sum[1, 0]), in_far0), 0)
        in_near0, small = xch_with(in_send0, small, "dp", 0)
        in_half1 = add(in_keep1, in_near1)
        in_far1 = xch(in_half1[0], "tensor", 1)
        g_in = jnp.stack([add(in_keep0, in_near0), add(in_half1[1], in_far1)])
        for bit in range(1, bits):
            keep, send = parts(g_in, bit)
            got, small = xch_with(send, small, "dp", bit)
            g_in = add(keep, got)

        grad_patches = jnp.stack([pair, other], axis=1)
        flip_c = bit_of("tensor", 0)
        flip_y = bit_of("tensor", 1)
        grad_patches = jnp.where(flip_c, grad_patches[:, ::-1], grad_patches)
        grad_patches = jnp.where(flip_y, grad_patches[::-1], grad_patches)
        grad_patches = grad_patches.reshape(patch_embeds.shape)

        g_fc = g_fc.reshape(2, rows, width).astype(F32)
        g_in = g_in.reshape(2, rows, half)
        g_in = jnp.concatenate([g_in[0], g_in[1]], axis=1).astype(F32)
        small = small.astype(F32)
        six = lax.dynamic_slice_in_dim(small[:6], me_d * rows, rows, 1)
        lanes = lax.dynamic_index_in_dim(small[8:].reshape(4, 2 * width), me_t, 0, keepdims=False)
        g_b1 = lanes[:width].reshape(-1, HD)
        g_bh = lanes[width : width + 3 * hw].reshape(-1, HD)
        g_b1 = lax.dynamic_slice_in_dim(g_b1, me_d * per, per, 1)
        g_bh = lax.dynamic_slice_in_dim(g_bh, me_d * per, per, 1)
        return (
            block_out,
            grad_patches,
            six[0],
            six[1],
            g_in[:, :hw],
            g_in[:, hw : 2 * hw],
            g_in[:, 2 * hw : 3 * hw],
            g_bh[:heads],
            g_bh[2 * heads :],
            g_in[:, 3 * hw :].T,
            six[4],
            six[2],
            six[3],
            g_fc[0],
            g_b1,
            g_fc[1].T,
            six[5],
        )

    return body


def solution(mesh):
    strip = P("dp", None, None)
    row_cut = P("dp", "tensor")
    col_cut = P("tensor", "dp")
    vector = P("dp")
    return jax.shard_map(
        make_body(mesh),
        mesh=mesh,
        in_specs=(
            strip,
            P("dp", None),
            strip,
            vector,
            vector,
            row_cut,
            row_cut,
            row_cut,
            col_cut,
            col_cut,
            col_cut,
            vector,
            vector,
            vector,
            row_cut,
            col_cut,
            col_cut,
            vector,
        ),
        out_specs=(
            strip,
            strip,
            vector,
            vector,
            row_cut,
            row_cut,
            row_cut,
            col_cut,
            col_cut,
            col_cut,
            vector,
            vector,
            vector,
            row_cut,
            col_cut,
            col_cut,
            vector,
        ),
        check_vma=False,
    )
```

```python
import functools

import jax
import jax.numpy as jnp
from jax import lax
from jax.experimental import pallas as pl
from jax.experimental.pallas import tpu as pltpu
from jax.sharding import PartitionSpec as P

HD = 64
EPS = 1e-06
BIG = 2.0**100
BF = jnp.bfloat16
F32 = jnp.float32
VEC = 8
COST = 20
VMEM_LIMIT = 48 * 1024 * 1024


def nn(a, b):
    return lax.dot_general(a, b, (((1,), (0,)), ((), ())), preferred_element_type=F32)


def nt(a, b):
    return lax.dot_general(a, b, (((1,), (1,)), ((), ())), preferred_element_type=F32)


def tn(a, b):
    return lax.dot_general(a, b, (((0,), (0,)), ((), ())), preferred_element_type=F32)


def norm_parts(v):
    c = v - jnp.mean(v, axis=-1, keepdims=True)
    rstd = lax.rsqrt(jnp.mean(c * c, axis=-1, keepdims=True) + EPS)
    return c * rstd, rstd


def norm_back(grad, gain, xhat, rstd):
    scaled = grad * gain
    m1 = jnp.mean(scaled, axis=-1, keepdims=True)
    m2 = jnp.mean(scaled * xhat, axis=-1, keepdims=True)
    return rstd * (scaled - m1 - xhat * m2)


def colsum(v):
    return jnp.sum(v, axis=0, keepdims=True)


def take_block(step, a_ref, b_ref, scr):
    @pl.when(step == 0)
    def _():
        scr[...] = a_ref[...]

    @pl.when(step == 1)
    def _():
        scr[...] = b_ref[...]


def attend_block(rows, heads, n1, scr, seg_ref, vec_ref, qe_ref, ke_ref, ve_ref, e_ref, att_ref, inv_ref):
    width = scr.shape[2]
    hw = heads * HD
    w = scr[:, :rows, :].reshape(width, width)
    vec = jnp.sum(scr[:, rows:, :].astype(F32), axis=0)
    vec_ref[0] = vec
    length = n1.shape[0]
    proj = nn(n1, w[:, : 3 * hw])
    bq = vec[7:8, :hw]
    bv = vec[7:8, hw : 2 * hw]
    q = ((proj[:, :hw] + bq).astype(BF).astype(F32) * (HD**-0.5)).astype(BF)
    k = proj[:, hw : 2 * hw].astype(BF)
    v = (proj[:, 2 * hw :] + bv).astype(BF)
    lane = lax.broadcasted_iota(jnp.int32, (length, HD), 1)
    hot = jnp.where(lane == seg_ref[...], 1.0, 0.0)
    ext_k = jnp.where(lane < 4, hot, 0.0).astype(BF)
    ext_q = jnp.where(lane < 4, (hot - 1.0) * BIG, 0.0).astype(BF)
    ext_v = jnp.where(lane < 2, 1.0, 0.0).astype(BF)
    atts = [jnp.zeros((length, HD), BF)]
    invs = [jnp.zeros((length, HD), F32)]
    for h in range(heads):
        cut = slice(h * HD, (h + 1) * HD)
        qe = jnp.concatenate([q[:, cut], ext_q], axis=1)
        ke = jnp.concatenate([k[:, cut], ext_k], axis=1)
        ve = jnp.concatenate([v[:, cut], ext_v], axis=1)
        qe_ref[0, h] = qe
        ke_ref[0, h] = ke
        ve_ref[0, h] = ve
        s = nt(ke, qe)
        e = jnp.exp(s - jnp.max(s, axis=0, keepdims=True)).astype(BF)
        e_ref[0, h] = e
        o = tn(e, ve)
        inv = 1.0 / o[:, HD : HD + 1]
        atts.append((o[:, :HD] * inv).astype(BF))
        invs.append(jnp.broadcast_to(inv, (length, HD)))
    att = jnp.concatenate(atts, axis=1)
    att_ref[0] = att
    inv_ref[0] = jnp.concatenate(invs, axis=1)
    return nt(att, w[:, 3 * hw - HD :])


def attn_fwd_first(rows, heads, x_ref, seg_ref, a_ref, b_ref, n1_ref, part_ref, vec_ref, qe_ref, ke_ref, ve_ref, e_ref, att_ref, inv_ref, scr):
    step = pl.program_id(0)
    take_block(step, a_ref, b_ref, scr)

    @pl.when(step == 0)
    def _():
        vec = jnp.sum(a_ref[:, rows:, :].astype(F32), axis=0)
        xhat, _ = norm_parts(x_ref[...].astype(F32))
        n1_ref[...] = (xhat * vec[0:1] + vec[1:2]).astype(BF)
        part_ref[...] = jnp.zeros_like(part_ref)

    part_ref[...] += attend_block(rows, heads, n1_ref[...], scr, seg_ref, vec_ref, qe_ref, ke_ref, ve_ref, e_ref, att_ref, inv_ref)


def attn_fwd_second(rows, heads, x_ref, n1_ref, part_ref, dvec_ref, seg_ref, a_ref, b_ref, k0, k1, k2, k3, k4, k5, k6, mid_ref, n2_ref, vec_ref, qe_ref, ke_ref, ve_ref, e_ref, att_ref, inv_ref, scr):
    step = pl.program_id(0)
    take_block(step, a_ref, b_ref, scr)
    more = attend_block(rows, heads, n1_ref[...], scr, seg_ref, vec_ref, qe_ref, ke_ref, ve_ref, e_ref, att_ref, inv_ref)

    @pl.when(step == 0)
    def _():
        mid_ref[...] = x_ref[...].astype(F32) + dvec_ref[0, 4:5] + part_ref[...] + more

    @pl.when(step == 1)
    def _():
        middle = mid_ref[...] + more
        mid_ref[...] = middle
        xhat, _ = norm_parts(middle)
        n2_ref[...] = (xhat * dvec_ref[0, 2:3] + dvec_ref[0, 3:4]).astype(BF)


def gelu_both(x):
    z = jnp.abs(x) * (0.5**0.5)
    t = 1.0 / (1.0 + 0.3275911 * z)
    gauss = jnp.exp(x * x * -0.5)
    poly = t * (0.254829592 + t * (-0.284496736 + t * (1.421413741 + t * (-1.453152027 + t * 1.061405429))))
    tail = 0.5 * poly * gauss
    cdf = jnp.where(x < 0, tail, 1.0 - tail)
    return x * cdf, cdf + x * gauss * 0.3989422804014327


CHUNKS = 3


def mlp_chunk(rows, n2_ref, dy_ref, n2t, dyt, w_ref, b1_ref, g_ref, gbias_ref):
    chunk = w_ref.shape[3]
    width = n2t.shape[0]
    w1 = w_ref[:, 0, :rows, :].reshape(width, chunk)
    w2 = w_ref[:, 0, rows:, :].reshape(width, chunk)
    pre = nn(n2_ref[...], w1) + b1_ref[0, 6:7]
    hid, slope = gelu_both(pre)
    hid = hid.astype(BF)
    gpre = (nn(dy_ref[...], w2) * slope).astype(BF)
    gbias_ref[0, 0:1] = colsum(gpre.astype(F32))
    g_ref[:, :chunk] = nn(n2t[...], gpre).astype(BF)
    g_ref[:, chunk:] = nn(dyt[...], hid).astype(BF)
    return nt(hid, w2), nt(gpre, w1)


def mlp_steps(rows, n2_ref, dy_ref, w_ref, b1_ref, g_refs, gbias_ref, n2t, dyt, first, accumulate):
    step = pl.program_id(0)

    @pl.when(step == 0)
    def _():
        n2t[...] = n2_ref[...].T
        dyt[...] = dy_ref[...].T
        first()

    for i, g_ref in enumerate(g_refs):

        @pl.when(step // CHUNKS == i)
        def _():
            accumulate(*mlp_chunk(rows, n2_ref, dy_ref, n2t, dyt, w_ref, b1_ref, g_ref, gbias_ref))


def mlp_first(rows, ids_ref, n2_ref, dy_ref, w_ref, b1_ref, out_ref, back_ref, g0_ref, g1_ref, gbias_ref, n2t, dyt):
    def first():
        out_ref[...] = jnp.zeros_like(out_ref)
        back_ref[...] = jnp.zeros_like(back_ref)

    def accumulate(out, back):
        out_ref[...] += out
        back_ref[...] += back

    mlp_steps(rows, n2_ref, dy_ref, w_ref, b1_ref, (g0_ref, g1_ref), gbias_ref, n2t, dyt, first, accumulate)


def mlp_second(rows, ids_ref, n2_ref, dy_ref, w_ref, b1_ref, out0_ref, back0_ref, mid_ref, dvec_ref, y_ref, gm_ref, gml_ref, vg_ref, g0_ref, g1_ref, gbias_ref, n2t, dyt, out_ref, back_ref):
    def first():
        out_ref[...] = out0_ref[...]
        back_ref[...] = back0_ref[...]

    def accumulate(out, back):
        out_ref[...] += out
        back_ref[...] += back

    mlp_steps(rows, n2_ref, dy_ref, w_ref, b1_ref, (g0_ref, g1_ref), gbias_ref, n2t, dyt, first, accumulate)

    @pl.when(pl.program_id(0) == 2 * CHUNKS - 1)
    def _():
        middle = mid_ref[...]
        dy = dy_ref[...].astype(F32)
        y_ref[...] = (middle + out_ref[...] + dvec_ref[0, 5:6]).astype(BF)
        grad = back_ref[...]
        xhat, rstd = norm_parts(middle)
        gm = dy + norm_back(grad, dvec_ref[0, 2:3], xhat, rstd)
        gm_ref[...] = gm
        gml_ref[...] = gm.astype(BF)
        vg_ref[0:1] = colsum(grad * xhat)
        vg_ref[1:2] = colsum(grad)
        vg_ref[2:3] = colsum(gm)
        vg_ref[3:4] = colsum(dy)


def attend_back(rows, heads, n1, gml, scr, qe_ref, ke_ref, ve_ref, e_ref, att_ref, inv_ref, ga_ref, gb_ref):
    width = scr.shape[2]
    hw = heads * HD
    half = width // 2
    w = scr[:, :rows, :].reshape(width, width)
    length = n1.shape[0]
    att = att_ref[0]
    ga = nn(gml, w[:, 3 * hw - HD :]).astype(BF).astype(F32) * inv_ref[0]
    do = ga.astype(BF)
    prod = do.astype(F32) * att.astype(F32)
    lane = lax.broadcasted_iota(jnp.int32, (length, HD), 1)
    dqs, dks, dvs = [], [], []
    for h in range(heads):
        cut = slice((h + 1) * HD, (h + 2) * HD)
        delta = -jnp.sum(prod[:, cut], axis=1, keepdims=True)
        high = delta.astype(BF).astype(F32)
        ext = jnp.where(lane == 0, high, jnp.where(lane == 1, delta - high, 0.0)).astype(BF)
        doe = jnp.concatenate([do[:, cut], ext], axis=1)
        e = e_ref[0, h]
        dp = nt(ve_ref[0, h], doe)
        ds = (e.astype(F32) * dp).astype(BF)
        dqs.append((tn(ds, ke_ref[0, h])[:, :HD] * (HD**-0.5)).astype(BF))
        dks.append(nn(ds, qe_ref[0, h][:, :HD]).astype(BF))
        dvs.append(nn(e, do[:, cut]).astype(BF))
    dqkv = jnp.concatenate(dqs + dks + dvs, axis=1)
    last = jnp.concatenate([dvs[-1], jnp.zeros((length, hw), BF)], axis=1)
    split = 3 * hw - HD
    ga_ref[0] = tn(n1, dqkv[:, :half]).astype(BF)
    gb_ref[0, :, : split - half] = tn(n1, dqkv[:, half:split]).astype(BF)
    gb_ref[0, :, split - half :] = (tn(n1, last) + tn(gml, att)).astype(BF)
    return nt(dqkv, w[:, : 3 * hw]), colsum(dqkv.astype(F32))


def attn_back_first(rows, heads, n1_ref, gml_ref, a_ref, b_ref, qe_ref, ke_ref, ve_ref, e_ref, att_ref, inv_ref, back_ref, ga_ref, gb_ref, gbias_ref, scr):
    step = pl.program_id(0)
    take_block(step, a_ref, b_ref, scr)
    back, gbias_ref[0, 0:1] = attend_back(rows, heads, n1_ref[...], gml_ref[...], scr, qe_ref, ke_ref, ve_ref, e_ref, att_ref, inv_ref, ga_ref, gb_ref)

    @pl.when(step == 0)
    def _():
        back_ref[...] = back

    @pl.when(step == 1)
    def _():
        back_ref[...] += back


def attn_back_second(rows, heads, n1_ref, gml_ref, a_ref, b_ref, qe_ref, ke_ref, ve_ref, e_ref, att_ref, inv_ref, x_ref, gm_ref, back0_ref, dvec_ref, me_ref, vg2_ref, hid_a_ref, hid_b_ref, head_b_ref, gx_ref, small_ref, ga_ref, gb_ref, scr, back_ref, rows_ref):
    step = pl.program_id(0)
    take_block(step, a_ref, b_ref, scr)
    back, bias = attend_back(rows, heads, n1_ref[...], gml_ref[...], scr, qe_ref, ke_ref, ve_ref, e_ref, att_ref, inv_ref, ga_ref, gb_ref)
    me = me_ref[0]

    def row_of(block):
        return 8 + 2 * (me ^ block)

    @pl.when(step == 0)
    def _():
        back_ref[...] = back0_ref[...] + back
        rows_ref[...] = jnp.zeros_like(rows_ref)
        rows_ref[2:6] = vg2_ref[...]
        for block, ref, at in ((3, hid_b_ref, 0), (2, hid_b_ref, 1), (1, hid_a_ref, 0), (0, hid_a_ref, 1)):
            rows_ref[pl.ds(row_of(block), 1)] = ref[at]
        for block, value in ((3, head_b_ref[0]), (1, head_b_ref[1]), (2, bias)):
            rows_ref[pl.ds(row_of(block) + 1, 1), : value.shape[1]] = value

    @pl.when(step == 1)
    def _():
        grad = back_ref[...] + back
        xhat, rstd = norm_parts(x_ref[...].astype(F32))
        gx_ref[...] = (gm_ref[...] + norm_back(grad, dvec_ref[0, 0:1], xhat, rstd)).astype(BF)
        rows_ref[0:1] = colsum(grad * xhat)
        rows_ref[1:2] = colsum(grad)
        rows_ref[pl.ds(row_of(0) + 1, 1), : bias.shape[1]] = bias
        small_ref[...] = rows_ref[...].astype(BF)


def whole_block(shape):
    return pl.BlockSpec(shape, lambda *_: (0,) * len(shape))


def step_block(shape, first, stride):
    rest = (0,) * (len(shape) - 1)
    return pl.BlockSpec((1,) + shape[1:], lambda i, *_: (first + stride * i,) + rest)


def call(kernel, args, in_kinds, outs, out_kinds, scratch, flops, order=(0, 1), out_order=None, aliases=None):
    def make(order):
        return {
            "w": whole_block,
            "s": lambda shape: step_block(shape, order[0], order[1] - order[0]),
            "a": lambda shape: pl.BlockSpec(memory_space=pl.ANY),
            "c": lambda shape: pl.BlockSpec(memory_space=pltpu.SMEM),
        }

    ins = make(order)
    out_specs = make(out_order or order)
    moved = sum(a.size * a.dtype.itemsize for a in args) + sum(o.size * o.dtype.itemsize for o in outs)
    return pl.pallas_call(
        kernel,
        grid=(2,),
        in_specs=[ins[kind](a.shape) for kind, a in zip(in_kinds, args)],
        out_specs=[out_specs[kind](o.shape) for kind, o in zip(out_kinds, outs)],
        out_shape=outs,
        scratch_shapes=scratch,
        input_output_aliases=aliases or {},
        compiler_params=pltpu.CompilerParams(vmem_limit_bytes=VMEM_LIMIT),
        cost_estimate=pl.CostEstimate(flops=flops * COST, bytes_accessed=moved, transcendentals=0),
    )(*args)


def total(*values):
    out = values[0].astype(F32)
    for value in values[1:]:
        out = out + value.astype(F32)
    return out.astype(BF)


def fc_early(part_a, bit_ref, mine, got, far_out, keep_out, send_out):
    bit = bit_ref[0]
    far_out[...] = total(mine[:, :, :, :part_a], got[:, :, :, :part_a])
    keep_out[0] = total(mine[0, bit, :, part_a:], got[0, bit, :, part_a:])
    send_out[0] = total(mine[0, 1 - bit, :, part_a:], got[0, 1 - bit, :, part_a:])


def fc_late(part_a, bit_ref, mine, got, far, keep2, near2, half_out, keep_out, send_out):
    bit = bit_ref[0]
    half_out[...] = total(keep2[...], near2[...])
    for which, out in ((bit, keep_out), (1 - bit, send_out)):
        out[0, :, :part_a] = total(mine[0, which, :, :part_a], got[0, which, :, :part_a], far[0, which])
        out[0, :, part_a:] = total(mine[0, which, :, part_a:], got[0, which, :, part_a:])


def in_first(bit_ref, mine_a, got_a, mine_b, got_b, far_out, own_out, keep_out, send_out):
    bit = bit_ref[0]
    far_out[...] = total(mine_a[0], got_a[0])
    own_out[...] = total(mine_a[1], got_a[1])
    for j in range(2):
        keep_out[j, 0] = total(mine_b[j, 0, bit], got_b[j, 0, bit])
        send_out[j, 0] = total(mine_b[j, 0, 1 - bit], got_b[j, 0, 1 - bit])


def by_pair(kernel, bit, args, outs):
    pairs = outs[0].shape[0]

    def spec(shape):
        at = 0 if shape[0] == pairs and (len(shape) == 3 or shape[1] == 2) else 1
        block = shape[:at] + (1,) + shape[at + 1 :]
        return pl.BlockSpec(block, lambda i, bit: (0,) * at + (i,) + (0,) * (len(shape) - at - 1))

    moved = sum(a.size * a.dtype.itemsize for a in args) + sum(o.size * o.dtype.itemsize for o in outs)
    return pl.pallas_call(
        kernel,
        grid_spec=pltpu.PrefetchScalarGridSpec(
            num_scalar_prefetch=1,
            grid=(pairs,),
            in_specs=[spec(a.shape) for a in args],
            out_specs=[spec(o.shape) for o in outs],
        ),
        out_shape=outs,
        compiler_params=pltpu.CompilerParams(vmem_limit_bytes=VMEM_LIMIT),
        cost_estimate=pl.CostEstimate(flops=0, bytes_accessed=moved, transcendentals=0),
    )(bit, *args)


def after(value, *others):
    return lax.optimization_barrier((value,) + others)[0]


def sds(shape, dtype):
    return jax.ShapeDtypeStruct(shape, dtype)


def make_body(mesh):
    nd = mesh.shape["dp"]
    nt_ax = mesh.shape["tensor"]
    bits = nd.bit_length() - 1

    def xch(v, axis, bit):
        n = mesh.shape[axis]
        return lax.ppermute(v, axis, [(i, i ^ (1 << bit)) for i in range(n)])

    def bit_of(axis, bit):
        return ((lax.axis_index(axis) >> bit) & 1) == 1

    def body(
        patch_embeds,
        segment_ids,
        cotangent,
        ln1_gain,
        ln1_bias,
        w_query,
        w_key,
        w_value,
        b_query,
        b_value,
        w_out,
        b_out,
        ln2_gain,
        ln2_bias,
        w_fc1,
        b_fc1,
        w_fc2,
        b_fc2,
    ):
        strips, length, width = patch_embeds.shape
        assert strips == nt_ax == 4
        rows = width // nd
        heads = b_query.shape[0]
        hw = heads * HD
        per = HD // nd
        me_t = lax.axis_index("tensor")
        me_d = lax.axis_index("dp")
        x = lax.dynamic_index_in_dim(patch_embeds, me_t, 0, keepdims=False)
        dy = lax.dynamic_index_in_dim(cotangent, me_t, 0, keepdims=False)
        seg = lax.dynamic_index_in_dim(segment_ids, me_t, 0, keepdims=False)[:, None]

        def place(v, total, at):
            wide = jnp.zeros(v.shape[:-1] + (total,), BF)
            return lax.dynamic_update_slice_in_dim(wide, v, at, v.ndim - 1)

        six = jnp.stack([ln1_gain, ln1_bias, ln2_gain, ln2_bias, b_out, b_fc2])
        six = place(six, width, me_d * rows)
        heads_vec = place(jnp.concatenate([b_query, b_value, b_fc1]), HD, me_d * per)
        vec = jnp.concatenate(
            [
                six,
                heads_vec[2 * heads :].reshape(1, width),
                jnp.pad(heads_vec[: 2 * heads].reshape(1, 2 * hw), ((0, 0), (0, width - 2 * hw))),
            ]
        )
        share1 = jnp.concatenate(
            [jnp.concatenate([w_query, w_key, w_value, w_out.T], axis=1), vec]
        )
        share2 = jnp.concatenate([w_fc1, w_fc2.T])
        fc = lax.all_gather(share2, ("dp", "tensor"), axis=0, tiled=False)
        fc = fc.reshape(nd, nt_ax, 2 * rows, width)

        def spread(v, bit, axis, wait=None):
            r = xch(v, "dp", bit)
            if wait is not None:
                r = after(r, wait)
            high = bit_of("dp", bit)
            return jnp.stack([jnp.where(high, r, v), jnp.where(high, v, r)], axis=axis)

        quarter = share1[None]
        for bit in reversed(range(1, bits)):
            quarter = spread(quarter, bit, 1).reshape(-1, rows + VEC, width)
        quarter = after(quarter, x, dy, seg)
        far = xch(quarter, "tensor", 1)
        v0 = spread(quarter, 0, 1, far).reshape(nd, rows + VEC, width)
        v1 = xch(v0, "tensor", 0)

        row32 = sds((length, width), F32)
        row16 = sds((length, width), BF)
        head = sds((4, heads, length, 2 * HD), BF)
        kept = [
            sds((4, VEC, width), F32),
            head,
            head,
            head,
            sds((4, heads, length, length), BF),
            sds((4, length, width - 3 * hw + HD), BF),
            sds((4, length, width - 3 * hw + HD), F32),
        ]
        block_scr = pltpu.VMEM((nd, rows + VEC, width), BF)
        big = 2 * length * width * width
        att_flops = 2 * big + 4 * heads * length * length * 4 * HD
        n1, part, *kept_a = call(
            functools.partial(attn_fwd_first, rows, heads),
            [x, seg, v0, v1],
            "wwww",
            [row16, row32] + kept,
            "wwsssssss",
            [block_scr],
            att_flops,
        )
        dvec = kept_a[0]
        v2 = spread(far, 0, 1, part).reshape(nd, rows + VEC, width)
        v3 = xch(v2, "tensor", 0)
        middle, n2, *kept_b = call(
            functools.partial(attn_fwd_second, rows, heads),
            [x, n1, part, dvec, seg, v2, v3] + kept_a,
            "wwwwwww" + "a" * 7,
            [row32, row16] + kept,
            "wwsssssss",
            [block_scr],
            att_flops,
            out_order=(2, 3),
            aliases={7 + i: 2 + i for i in range(7)},
        )
        vec_all = kept_b[0]

        chunk = width // CHUNKS

        def mlp_call(kernel, n2, first, more, outs, scratch):
            ids = jnp.stack([me_t ^ first, me_t ^ (first - 1)])
            args = [n2, dy, fc, vec_all] + more
            specs = [
                whole_block(n2.shape),
                whole_block(dy.shape),
                pl.BlockSpec((nd, 1, 2 * rows, chunk), lambda i, ids: (0, ids[i // CHUNKS], 0, i % CHUNKS)),
                pl.BlockSpec((1, VEC, chunk), lambda i, ids: (first - i // CHUNKS, 0, i % CHUNKS)),
            ] + [whole_block(m.shape) for m in more]
            grad = sds((width, 2 * width), BF)
            return pl.pallas_call(
                kernel,
                grid_spec=pltpu.PrefetchScalarGridSpec(
                    num_scalar_prefetch=1,
                    grid=(2 * CHUNKS,),
                    in_specs=specs,
                    out_specs=[whole_block(o.shape) for o in outs]
                    + [
                        pl.BlockSpec((width, 2 * chunk), lambda i, ids: (0, jnp.minimum(i, CHUNKS - 1))),
                        pl.BlockSpec((width, 2 * chunk), lambda i, ids: (0, jnp.maximum(i - CHUNKS, 0))),
                        pl.BlockSpec((1, 1, chunk), lambda i, ids: (i // CHUNKS, 0, i % CHUNKS)),
                    ],
                    scratch_shapes=[pltpu.VMEM((width, length), BF)] * 2 + scratch,
                ),
                out_shape=outs + [grad, grad, sds((2, 1, width), F32)],
                compiler_params=pltpu.CompilerParams(vmem_limit_bytes=VMEM_LIMIT),
                cost_estimate=pl.CostEstimate(flops=12 * big * COST, bytes_accessed=20 * 2**20, transcendentals=0),
            )(ids, *args)

        def add(a, b):
            return (a.astype(F32) + b.astype(F32)).astype(BF)

        def parts(v, bit):
            high = bit_of("dp", bit)
            v = v.reshape(v.shape[:-3] + (v.shape[-3] // 2, 2) + v.shape[-2:])
            lo, hi = v[..., 0, :, :], v[..., 1, :, :]
            return jnp.where(high, hi, lo), jnp.where(high, lo, hi)

        def cut(v):
            return v.reshape(v.shape[:-2] + (nd, rows, v.shape[-1]))

        def add_parts(a, b, bit):
            keep_a, send_a = parts(a, bit)
            keep_b, send_b = parts(b, bit)
            return add(keep_a, keep_b), add(send_a, send_b)

        part_a = 2 * chunk
        part_b = 2 * width - part_a
        pairs = nd // 2
        bit0 = (me_d & 1).reshape(1)

        def paired(v):
            return v.reshape(v.shape[:-2] + (pairs, 2, rows, v.shape[-1]))

        def whole_pairs(c):
            return sds((pairs, 2, rows, c), BF)

        def half_pairs(c):
            return sds((pairs, rows, c), BF)

        out_b, back_b, g3, g2, gb1_b = mlp_call(functools.partial(mlp_first, rows), n2, 3, [], [row32, row32], [])
        got_fc = xch(g3, "tensor", 0)
        fc_send0, fc_keep2, fc_send2 = by_pair(
            functools.partial(fc_early, part_a),
            bit0,
            [paired(g2), paired(got_fc)],
            [whole_pairs(part_a), half_pairs(part_b), half_pairs(part_b)],
        )
        fc_far0 = xch(fc_send0, "tensor", 1)
        fc_near2 = xch(fc_send2, "dp", 0)
        y, gm, gml, vg2, g1, g0, gb1_a = mlp_call(
            functools.partial(mlp_second, rows),
            after(n2, fc_send0, fc_send2),
            1,
            [out_b, back_b, middle, dvec],
            [row16, row32, row16, sds((4, width), F32)],
            [pltpu.VMEM((length, width), F32)] * 2,
        )
        y_far = xch(y, "tensor", 1)
        y_core = xch(y, "tensor", 0)
        got_fc = xch(g1, "tensor", 0)
        gml, fc_far0, fc_near2 = lax.optimization_barrier((gml, fc_far0, fc_near2))

        g_in = sds((2, width, width // 2), BF)
        gb_in = sds((2, 1, 3 * hw), F32)
        back_flops = 4 * big + 10 * heads * length * length * 4 * HD
        saved = kept_b[1:]
        back1, in_a31, in_b31, gbh_b = call(
            functools.partial(attn_back_first, rows, heads),
            [n1, gml, v3, v1] + saved,
            "wwww" + "ssssss",
            [row32, g_in, g_in, gb_in],
            "wsss",
            [block_scr],
            back_flops,
            order=(3, 1),
            out_order=(0, 1),
        )
        got_ia = xch(in_a31, "tensor", 0)
        got_ib = xch(in_b31, "tensor", 0)
        got_fc = after(got_fc, back1)
        fc_half2, fc_keep, fc_send = by_pair(
            functools.partial(fc_late, part_a),
            bit0,
            [paired(g0), paired(got_fc), fc_far0, fc_keep2, fc_near2],
            [half_pairs(part_b), half_pairs(2 * width), half_pairs(2 * width)],
        )
        fc_far1 = xch(fc_half2, "tensor", 1)
        fc_near = xch(fc_send, "dp", 0)
        gml, y_far, y_core = lax.optimization_barrier((gml, y_far, y_core, fc_half2, fc_send))[:3]
        y_both = xch(y_far, "tensor", 0)
        gx, small, in_a20, in_b20 = call(
            functools.partial(attn_back_second, rows, heads),
            [n1, gml, v2, v0] + saved + [x, gm, back1, dvec, me_t.reshape(1), vg2, gb1_a, gb1_b, gbh_b],
            "wwww" + "ssssss" + "wwww" + "cwwww",
            [row16, sds((16, width), BF), g_in, g_in],
            "wwss",
            [block_scr, pltpu.VMEM((length, width), F32), pltpu.VMEM((16, width), F32)],
            back_flops,
            order=(2, 0),
            out_order=(0, 1),
        )

        half = width // 2
        n_small = 2 * small.shape[0]

        def with_small(v, small):
            return jnp.concatenate([v.reshape(-1, half), small.reshape(n_small, half)])

        def split_small(got, small, shape):
            return got[:-n_small].reshape(shape), add(small, got[-n_small:].reshape(small.shape))

        got_ia, got_ib, fc_far1, y_both = lax.optimization_barrier((got_ia, got_ib, fc_far1, y_both))
        in_c = width // 2
        in_send0, in_own, in_keep1, in_send1 = by_pair(
            in_first,
            bit0,
            [paired(in_a20), paired(got_ia), paired(in_b20), paired(got_ib)],
            [whole_pairs(in_c), whole_pairs(in_c), sds((2, pairs, rows, in_c), BF), sds((2, pairs, rows, in_c), BF)],
        )
        in_near1 = xch(in_send1, "dp", 0)
        in_far0 = xch(with_small(in_send0, small), "tensor", 1)

        fc_near, fc_far1 = lax.optimization_barrier((fc_near, fc_far1, in_send0))[:2]
        g_fc = total(fc_keep, fc_near, jnp.pad(fc_far1, ((0, 0), (0, 0), (part_a, 0))))
        for bit in range(1, bits):
            keep, send = parts(g_fc, bit)
            g_fc = add(keep, xch(send, "dp", bit))

        gx_core = xch(gx, "tensor", 0)
        gx, in_far0 = lax.optimization_barrier((gx, in_far0))
        in_far0, small = split_small(in_far0, small, (nd, rows, half))
        in_keep0, in_send0 = parts(add(in_own.reshape(in_far0.shape), in_far0), 0)
        y = after(y, in_send0)
        got = xch(with_small(in_send0, small), "dp", 0)
        in_near0, small = split_small(got, small, in_send0.shape)
        in_half1 = add(in_keep1, in_near1)
        in_far1 = xch(in_half1[0], "tensor", 1)
        g_in = jnp.stack([add(in_keep0, in_near0), add(in_half1[1], in_far1)])
        gx_far = xch(gx, "tensor", 1)
        for bit in range(1, bits):
            keep, send = parts(g_in, bit)
            if bit == bits - 1:
                gx_far = after(gx_far, send)
                gx_both = xch(gx_far, "tensor", 0)
            got, small = split_small(xch(with_small(send, small), "dp", bit), small, send.shape)
            if bit == bits - 1:
                got, gx_both, gx_core = lax.optimization_barrier((got, gx_both, gx_core))
            g_in = add(keep, got)

        flip_c = bit_of("tensor", 0)
        flip_y = bit_of("tensor", 1)

        def strips_of(own, core, far, both):
            near = jnp.where(flip_c, core, own), jnp.where(flip_c, own, core)
            away = jnp.where(flip_c, both, far), jnp.where(flip_c, far, both)
            first = [jnp.where(flip_y, a, n) for n, a in zip(near, away)]
            second = [jnp.where(flip_y, n, a) for n, a in zip(near, away)]
            return jnp.stack(first + second)

        block_out = strips_of(y, y_core, y_far, y_both)
        grad_patches = strips_of(gx, gx_core, gx_far, gx_both)

        small = add(small, xch(small, "tensor", 0))
        g_fc = g_fc.reshape(rows, CHUNKS, 2, chunk).astype(F32)
        g_in = g_in.reshape(2, rows, half)
        g_in = jnp.concatenate([g_in[0], g_in[1]], axis=1).astype(F32)
        small = small.astype(F32)
        six = lax.dynamic_slice_in_dim(small[:6], me_d * rows, rows, 1)
        lanes = lax.dynamic_index_in_dim(small[8:].reshape(4, 2 * width), me_t, 0, keepdims=False)
        g_b1 = lanes[:width].reshape(-1, HD)
        g_bh = lanes[width : width + 3 * hw].reshape(-1, HD)
        g_b1 = lax.dynamic_slice_in_dim(g_b1, me_d * per, per, 1)
        g_bh = lax.dynamic_slice_in_dim(g_bh, me_d * per, per, 1)
        return (
            block_out,
            grad_patches,
            six[0],
            six[1],
            g_in[:, :hw],
            g_in[:, hw : 2 * hw],
            g_in[:, 2 * hw : 3 * hw],
            g_bh[:heads],
            g_bh[2 * heads :],
            g_in[:, 3 * hw :].T,
            six[4],
            six[2],
            six[3],
            g_fc[:, :, 0].reshape(rows, width),
            g_b1,
            g_fc[:, :, 1].reshape(rows, width).T,
            six[5],
        )

    return body


def solution(mesh):
    strip = P("dp", None, None)
    row_cut = P("dp", "tensor")
    col_cut = P("tensor", "dp")
    vector = P("dp")
    return jax.shard_map(
        make_body(mesh),
        mesh=mesh,
        in_specs=(
            strip,
            P("dp", None),
            strip,
            vector,
            vector,
            row_cut,
            row_cut,
            row_cut,
            col_cut,
            col_cut,
            col_cut,
            vector,
            vector,
            vector,
            row_cut,
            col_cut,
            col_cut,
            vector,
        ),
        out_specs=(
            strip,
            strip,
            vector,
            vector,
            row_cut,
            row_cut,
            row_cut,
            col_cut,
            col_cut,
            col_cut,
            vector,
            vector,
            vector,
            row_cut,
            col_cut,
            col_cut,
            vector,
        ),
        check_vma=False,
    )
```

```python
import functools

import jax
import jax.numpy as jnp
from jax import lax
from jax.experimental import pallas as pl
from jax.experimental.pallas import tpu as pltpu
from jax.sharding import PartitionSpec as P

HD = 64
EPS = 1e-06
BIG = 2.0**100
BF = jnp.bfloat16
F32 = jnp.float32
VEC = 8
SMALL = 16
COST = 20
VMEM_LIMIT = 48 * 1024 * 1024


def nn(a, b):
    return lax.dot_general(a, b, (((1,), (0,)), ((), ())), preferred_element_type=F32)


def nt(a, b):
    return lax.dot_general(a, b, (((1,), (1,)), ((), ())), preferred_element_type=F32)


def tn(a, b):
    return lax.dot_general(a, b, (((0,), (0,)), ((), ())), preferred_element_type=F32)


def norm_parts(v):
    c = v - jnp.mean(v, axis=-1, keepdims=True)
    rstd = lax.rsqrt(jnp.mean(c * c, axis=-1, keepdims=True) + EPS)
    return c * rstd, rstd


def norm_back(grad, gain, xhat, rstd):
    scaled = grad * gain
    m1 = jnp.mean(scaled, axis=-1, keepdims=True)
    m2 = jnp.mean(scaled * xhat, axis=-1, keepdims=True)
    return rstd * (scaled - m1 - xhat * m2)


def colsum(v):
    return jnp.sum(v, axis=0, keepdims=True)


def take_block(step, a_ref, b_ref, scr):
    @pl.when(step == 0)
    def _():
        scr[...] = a_ref[...]

    @pl.when(step == 1)
    def _():
        scr[...] = b_ref[...]


def attend_block(rows, heads, n1, scr, seg_ref, vec_ref, qe_ref, ke_ref, ve_ref, e_ref, att_ref, inv_ref):
    width = scr.shape[2]
    hw = heads * HD
    w = scr[:, :rows, :].reshape(width, width)
    vec = jnp.sum(scr[:, rows:, :].astype(F32), axis=0)
    vec_ref[0] = vec
    length = n1.shape[0]
    proj = nn(n1, w[:, : 3 * hw])
    bq = vec[7:8, :hw]
    bv = vec[7:8, hw : 2 * hw]
    q = ((proj[:, :hw] + bq).astype(BF).astype(F32) * (HD**-0.5)).astype(BF)
    k = proj[:, hw : 2 * hw].astype(BF)
    v = (proj[:, 2 * hw :] + bv).astype(BF)
    lane = lax.broadcasted_iota(jnp.int32, (length, HD), 1)
    hot = jnp.where(lane == seg_ref[...], 1.0, 0.0)
    ext_k = jnp.where(lane < 4, hot, 0.0).astype(BF)
    ext_q = jnp.where(lane < 4, (hot - 1.0) * BIG, 0.0).astype(BF)
    ext_v = jnp.where(lane < 2, 1.0, 0.0).astype(BF)
    atts = [jnp.zeros((length, HD), BF)]
    invs = [jnp.zeros((length, HD), F32)]
    for h in range(heads):
        cut = slice(h * HD, (h + 1) * HD)
        qe = jnp.concatenate([q[:, cut], ext_q], axis=1)
        ke = jnp.concatenate([k[:, cut], ext_k], axis=1)
        ve = jnp.concatenate([v[:, cut], ext_v], axis=1)
        qe_ref[0, h] = qe
        ke_ref[0, h] = ke
        ve_ref[0, h] = ve
        s = nt(ke, qe)
        e = jnp.exp(s - jnp.max(s, axis=0, keepdims=True)).astype(BF)
        e_ref[0, h] = e
        o = tn(e, ve)
        inv = 1.0 / o[:, HD : HD + 1]
        atts.append((o[:, :HD] * inv).astype(BF))
        invs.append(jnp.broadcast_to(inv, (length, HD)))
    att = jnp.concatenate(atts, axis=1)
    att_ref[0] = att
    inv_ref[0] = jnp.concatenate(invs, axis=1)
    return nt(att, w[:, 3 * hw - HD :])


def attn_fwd_first(rows, heads, x_ref, seg_ref, a_ref, b_ref, n1_ref, part_ref, vec_ref, qe_ref, ke_ref, ve_ref, e_ref, att_ref, inv_ref, scr):
    step = pl.program_id(0)
    take_block(step, a_ref, b_ref, scr)

    @pl.when(step == 0)
    def _():
        vec = jnp.sum(a_ref[:, rows:, :].astype(F32), axis=0)
        xhat, _ = norm_parts(x_ref[...].astype(F32))
        n1_ref[...] = (xhat * vec[0:1] + vec[1:2]).astype(BF)
        part_ref[...] = jnp.zeros_like(part_ref)

    part_ref[...] += attend_block(rows, heads, n1_ref[...], scr, seg_ref, vec_ref, qe_ref, ke_ref, ve_ref, e_ref, att_ref, inv_ref)


def attn_fwd_second(rows, heads, x_ref, n1_ref, part_ref, dvec_ref, seg_ref, a_ref, b_ref, k0, k1, k2, k3, k4, k5, k6, mid_ref, n2_ref, vec_ref, qe_ref, ke_ref, ve_ref, e_ref, att_ref, inv_ref, scr):
    step = pl.program_id(0)
    take_block(step, a_ref, b_ref, scr)
    more = attend_block(rows, heads, n1_ref[...], scr, seg_ref, vec_ref, qe_ref, ke_ref, ve_ref, e_ref, att_ref, inv_ref)

    @pl.when(step == 0)
    def _():
        mid_ref[...] = x_ref[...].astype(F32) + dvec_ref[0, 4:5] + part_ref[...] + more

    @pl.when(step == 1)
    def _():
        middle = mid_ref[...] + more
        mid_ref[...] = middle
        xhat, _ = norm_parts(middle)
        n2_ref[...] = (xhat * dvec_ref[0, 2:3] + dvec_ref[0, 3:4]).astype(BF)


def gelu_both(x):
    z = jnp.abs(x) * (0.5**0.5)
    t = 1.0 / (1.0 + 0.3275911 * z)
    gauss = jnp.exp(x * x * -0.5)
    poly = t * (0.254829592 + t * (-0.284496736 + t * (1.421413741 + t * (-1.453152027 + t * 1.061405429))))
    tail = 0.5 * poly * gauss
    cdf = jnp.where(x < 0, tail, 1.0 - tail)
    return x * cdf, cdf + x * gauss * 0.3989422804014327


CHUNKS = 3


def mlp_chunk(rows, n2_ref, dy_ref, n2t, dyt, w_ref, b1_ref, g_ref, gbias_ref):
    chunk = w_ref.shape[3]
    width = n2t.shape[0]
    w1 = w_ref[:, 0, :rows, :].reshape(width, chunk)
    w2 = w_ref[:, 0, rows:, :].reshape(width, chunk)
    pre = nn(n2_ref[...], w1) + b1_ref[0, 6:7]
    hid, slope = gelu_both(pre)
    hid = hid.astype(BF)
    gpre = (nn(dy_ref[...], w2) * slope).astype(BF)
    gbias_ref[0, 0:1] = colsum(gpre.astype(F32))
    g_ref[:, :chunk] = nn(n2t[...], gpre).astype(BF)
    g_ref[:, chunk:] = nn(dyt[...], hid).astype(BF)
    return nt(hid, w2), nt(gpre, w1)


def mlp_steps(rows, n2_ref, dy_ref, w_ref, b1_ref, g_refs, gbias_ref, n2t, dyt, first, accumulate):
    step = pl.program_id(0)

    @pl.when(step == 0)
    def _():
        n2t[...] = n2_ref[...].T
        dyt[...] = dy_ref[...].T
        first()

    for i, g_ref in enumerate(g_refs):

        @pl.when(step // CHUNKS == i)
        def _():
            accumulate(*mlp_chunk(rows, n2_ref, dy_ref, n2t, dyt, w_ref, b1_ref, g_ref, gbias_ref))


def mlp_first(rows, ids_ref, n2_ref, dy_ref, w_ref, b1_ref, out_ref, back_ref, g0_ref, g1_ref, gbias_ref, n2t, dyt):
    def first():
        out_ref[...] = jnp.zeros_like(out_ref)
        back_ref[...] = jnp.zeros_like(back_ref)

    def accumulate(out, back):
        out_ref[...] += out
        back_ref[...] += back

    mlp_steps(rows, n2_ref, dy_ref, w_ref, b1_ref, (g0_ref, g1_ref), gbias_ref, n2t, dyt, first, accumulate)


def mlp_second(rows, ids_ref, n2_ref, dy_ref, w_ref, b1_ref, out0_ref, back0_ref, mid_ref, dvec_ref, y_ref, gm_ref, gml_ref, vg_ref, g0_ref, g1_ref, gbias_ref, n2t, dyt, out_ref, back_ref):
    def first():
        out_ref[...] = out0_ref[...]
        back_ref[...] = back0_ref[...]

    def accumulate(out, back):
        out_ref[...] += out
        back_ref[...] += back

    mlp_steps(rows, n2_ref, dy_ref, w_ref, b1_ref, (g0_ref, g1_ref), gbias_ref, n2t, dyt, first, accumulate)

    @pl.when(pl.program_id(0) == 2 * CHUNKS - 1)
    def _():
        middle = mid_ref[...]
        dy = dy_ref[...].astype(F32)
        y_ref[...] = (middle + out_ref[...] + dvec_ref[0, 5:6]).astype(BF)
        grad = back_ref[...]
        xhat, rstd = norm_parts(middle)
        gm = dy + norm_back(grad, dvec_ref[0, 2:3], xhat, rstd)
        gm_ref[...] = gm
        gml_ref[...] = gm.astype(BF)
        vg_ref[0:1] = colsum(grad * xhat)
        vg_ref[1:2] = colsum(grad)
        vg_ref[2:3] = colsum(gm)
        vg_ref[3:4] = colsum(dy)


def attend_back(rows, heads, n1, gml, scr, qe_ref, ke_ref, ve_ref, e_ref, att_ref, inv_ref, ga_ref, gb_ref):
    width = scr.shape[2]
    hw = heads * HD
    half = width // 2
    w = scr[:, :rows, :].reshape(width, width)
    length = n1.shape[0]
    att = att_ref[0]
    ga = nn(gml, w[:, 3 * hw - HD :]).astype(BF).astype(F32) * inv_ref[0]
    do = ga.astype(BF)
    prod = do.astype(F32) * att.astype(F32)
    lane = lax.broadcasted_iota(jnp.int32, (length, HD), 1)
    dqs, dks, dvs = [], [], []
    for h in range(heads):
        cut = slice((h + 1) * HD, (h + 2) * HD)
        delta = -jnp.sum(prod[:, cut], axis=1, keepdims=True)
        high = delta.astype(BF).astype(F32)
        ext = jnp.where(lane == 0, high, jnp.where(lane == 1, delta - high, 0.0)).astype(BF)
        doe = jnp.concatenate([do[:, cut], ext], axis=1)
        e = e_ref[0, h]
        dp = nt(ve_ref[0, h], doe)
        ds = (e.astype(F32) * dp).astype(BF)
        dqs.append((tn(ds, ke_ref[0, h])[:, :HD] * (HD**-0.5)).astype(BF))
        dks.append(nn(ds, qe_ref[0, h][:, :HD]).astype(BF))
        dvs.append(nn(e, do[:, cut]).astype(BF))
    dqkv = jnp.concatenate(dqs + dks + dvs, axis=1)
    last = jnp.concatenate([dvs[-1], jnp.zeros((length, hw), BF)], axis=1)
    split = 3 * hw - HD
    ga_ref[0] = tn(n1, dqkv[:, :half]).astype(BF)
    gb_ref[0, :, : split - half] = tn(n1, dqkv[:, half:split]).astype(BF)
    gb_ref[0, :, split - half :] = (tn(n1, last) + tn(gml, att)).astype(BF)
    return nt(dqkv, w[:, : 3 * hw]), colsum(dqkv.astype(F32))


def attn_back_first(rows, heads, n1_ref, gml_ref, a_ref, b_ref, qe_ref, ke_ref, ve_ref, e_ref, att_ref, inv_ref, back_ref, ga_ref, gb_ref, gbias_ref, scr):
    step = pl.program_id(0)
    take_block(step, a_ref, b_ref, scr)
    back, gbias_ref[0, 0:1] = attend_back(rows, heads, n1_ref[...], gml_ref[...], scr, qe_ref, ke_ref, ve_ref, e_ref, att_ref, inv_ref, ga_ref, gb_ref)

    @pl.when(step == 0)
    def _():
        back_ref[...] = back

    @pl.when(step == 1)
    def _():
        back_ref[...] += back


def attn_back_second(rows, heads, n1_ref, gml_ref, a_ref, b_ref, qe_ref, ke_ref, ve_ref, e_ref, att_ref, inv_ref, x_ref, gm_ref, back0_ref, dvec_ref, me_ref, vg2_ref, hid_a_ref, hid_b_ref, head_b_ref, gx_ref, small_ref, ga_ref, gb_ref, scr, back_ref, rows_ref):
    step = pl.program_id(0)
    take_block(step, a_ref, b_ref, scr)
    back, bias = attend_back(rows, heads, n1_ref[...], gml_ref[...], scr, qe_ref, ke_ref, ve_ref, e_ref, att_ref, inv_ref, ga_ref, gb_ref)
    me = me_ref[0]

    def row_of(block):
        return 8 + 2 * (me ^ block)

    @pl.when(step == 0)
    def _():
        back_ref[...] = back0_ref[...] + back
        rows_ref[...] = jnp.zeros_like(rows_ref)
        rows_ref[2:6] = vg2_ref[...]
        for block, ref, at in ((3, hid_b_ref, 0), (2, hid_b_ref, 1), (1, hid_a_ref, 0), (0, hid_a_ref, 1)):
            rows_ref[pl.ds(row_of(block), 1)] = ref[at]
        for block, value in ((3, head_b_ref[0]), (1, head_b_ref[1]), (2, bias)):
            rows_ref[pl.ds(row_of(block) + 1, 1), : value.shape[1]] = value

    @pl.when(step == 1)
    def _():
        grad = back_ref[...] + back
        xhat, rstd = norm_parts(x_ref[...].astype(F32))
        gx_ref[...] = (gm_ref[...] + norm_back(grad, dvec_ref[0, 0:1], xhat, rstd)).astype(BF)
        rows_ref[0:1] = colsum(grad * xhat)
        rows_ref[1:2] = colsum(grad)
        rows_ref[pl.ds(row_of(0) + 1, 1), : bias.shape[1]] = bias
        half = rows_ref.shape[1] // 2
        small_ref[:SMALL] = rows_ref[:, :half].astype(BF)
        small_ref[SMALL:] = rows_ref[:, half:].astype(BF)


def whole_block(shape):
    return pl.BlockSpec(shape, lambda *_: (0,) * len(shape))


def step_block(shape, first, stride):
    rest = (0,) * (len(shape) - 1)
    return pl.BlockSpec((1,) + shape[1:], lambda i, *_: (first + stride * i,) + rest)


def call(kernel, args, in_kinds, outs, out_kinds, scratch, flops, order=(0, 1), out_order=None, aliases=None):
    def make(order):
        return {
            "w": whole_block,
            "s": lambda shape: step_block(shape, order[0], order[1] - order[0]),
            "a": lambda shape: pl.BlockSpec(memory_space=pl.ANY),
            "c": lambda shape: pl.BlockSpec(memory_space=pltpu.SMEM),
        }

    ins = make(order)
    out_specs = make(out_order or order)
    moved = sum(a.size * a.dtype.itemsize for a in args) + sum(o.size * o.dtype.itemsize for o in outs)
    return pl.pallas_call(
        kernel,
        grid=(2,),
        in_specs=[ins[kind](a.shape) for kind, a in zip(in_kinds, args)],
        out_specs=[out_specs[kind](o.shape) for kind, o in zip(out_kinds, outs)],
        out_shape=outs,
        scratch_shapes=scratch,
        input_output_aliases=aliases or {},
        compiler_params=pltpu.CompilerParams(vmem_limit_bytes=VMEM_LIMIT),
        cost_estimate=pl.CostEstimate(flops=flops * COST, bytes_accessed=moved, transcendentals=0),
    )(*args)


def total(*values):
    out = values[0].astype(F32)
    for value in values[1:]:
        out = out + value.astype(F32)
    return out.astype(BF)


def fc_early(part_a, bit_ref, mine, got, far_out, keep_out, send_out):
    bit = bit_ref[0]
    far_out[...] = total(mine[:, :, :, :part_a], got[:, :, :, :part_a])
    keep_out[0] = total(mine[0, bit, :, part_a:], got[0, bit, :, part_a:])
    send_out[0] = total(mine[0, 1 - bit, :, part_a:], got[0, 1 - bit, :, part_a:])


def fc_late(part_a, bit_ref, mine, got, far, keep2, near2, half_out, keep_out, send_out):
    bit = bit_ref[0]
    half_out[...] = total(keep2[...], near2[...])
    for which, out in ((bit, keep_out), (1 - bit, send_out)):
        out[0, :, :part_a] = total(mine[0, which, :, :part_a], got[0, which, :, :part_a], far[0, which])
        out[0, :, part_a:] = total(mine[0, which, :, part_a:], got[0, which, :, part_a:])


def in_first(bit_ref, mine_a, got_a, mine_b, got_b, far_out, own_out, keep_out, send_out):
    bit = bit_ref[0]
    far_out[...] = total(mine_a[0], got_a[0])
    own_out[...] = total(mine_a[1], got_a[1])
    for j in range(2):
        keep_out[j, 0] = total(mine_b[j, 0, bit], got_b[j, 0, bit])
        send_out[j, 0] = total(mine_b[j, 0, 1 - bit], got_b[j, 0, 1 - bit])


def fc_split(part_a, bit_ref, keep, near, far, keep_out, send_out):
    bit = bit_ref[0]
    for which, out in ((bit, keep_out), (1 - bit, send_out)):
        out[0, :, :part_a] = total(keep[0, which, :, :part_a], near[0, which, :, :part_a])
        out[0, :, part_a:] = total(keep[0, which, :, part_a:], near[0, which, :, part_a:], far[0, which])


def rows_at(index, rows):
    return pl.ds(pl.multiple_of(index * rows, rows), rows)


def in_second(bit_ref, own, far, small, keep1, near1, pay_out, keep_out, far_out, own_out):
    bit = bit_ref[0]
    pairs, _, rows, _ = own.shape
    for i in range(pairs):
        keep, send = 2 * i + bit, 2 * i + 1 - bit
        keep_out[i] = total(own[i, bit], far[rows_at(keep, rows), :])
        pay_out[i * rows : (i + 1) * rows] = total(own[i, 1 - bit], far[rows_at(send, rows), :])
    pay_out[pairs * rows :] = total(small[...], far[2 * pairs * rows :])
    far_out[...] = total(keep1[0], near1[0])
    own_out[...] = total(keep1[1], near1[1])


def in_third(bit_ref, sent, keep_a, got, keep_b, far, pay_out, keep_out):
    bit = bit_ref[0]
    pairs, rows, _ = keep_a.shape
    n = pairs // 2
    for i in range(n):
        keep, send = 2 * i + bit, 2 * i + 1 - bit
        keep_out[0, i] = total(keep_a[keep], got[rows_at(keep, rows), :])
        keep_out[1, i] = total(keep_b[keep], far[keep])
        pay_out[i * rows : (i + 1) * rows] = total(keep_a[send], got[rows_at(send, rows), :])
        pay_out[(n + i) * rows : (n + i + 1) * rows] = total(keep_b[send], far[send])
    pay_out[pairs * rows :] = total(sent[pairs * rows :], got[pairs * rows :])


def in_next(bit_ref, sent, keep, got, pay_out, keep_out):
    bit = bit_ref[0]
    _, n, rows, _ = keep.shape
    m = n // 2
    for h in range(2):
        for i in range(m):
            stay, go = 2 * i + bit, 2 * i + 1 - bit
            keep_out[h, i] = total(keep[h, stay], got[rows_at(h * n + stay, rows), :])
            pay_out[(h * m + i) * rows : (h * m + i + 1) * rows] = total(keep[h, go], got[rows_at(h * n + go, rows), :])
    pay_out[2 * m * rows :] = total(sent[2 * n * rows :], got[2 * n * rows :])


def in_last(hw, bit_ref, sent, keep, got, q_out, k_out, v_out, o_out, small_out):
    rows = keep.shape[2]
    first = keep[0, 0].astype(F32) + got[:rows].astype(F32)
    second = keep[1, 0].astype(F32) + got[rows : 2 * rows].astype(F32)
    q_out[...] = first[:, :hw]
    k_out[...] = first[:, hw:]
    v_out[...] = second[:, :hw]
    o_out[...] = second[:, hw:].T
    small_out[...] = total(sent[2 * rows :], got[2 * rows :])


def small_last(me_ref, small, got, six_out, hidden_out, heads_out):
    me_t, me_d = me_ref[0], me_ref[1]
    both = small[...].astype(F32) + got[...].astype(F32)
    full = jnp.concatenate([both[:SMALL], both[SMALL:]], axis=1)
    width = full.shape[1]
    rows = six_out.shape[1]
    per = hidden_out.shape[1]

    def pick(values, count, wrap):
        lane = lax.broadcasted_iota(jnp.int32, (width, count), 0)
        at = lax.broadcasted_iota(jnp.int32, (width, count), 1) + me_d * count
        ones = jnp.where(lax.rem(lane, wrap) == at, 1.0, 0.0)
        return lax.dot_general(
            values, ones, (((1,), (0,)), ((), ())), precision=lax.Precision.HIGHEST, preferred_element_type=F32
        )

    six_out[...] = pick(full[:8], rows, width)
    row = lax.broadcasted_iota(jnp.int32, (SMALL, width), 0)
    for which, out in ((0, hidden_out), (1, heads_out)):
        mine = colsum(jnp.where(row == 8 + 2 * me_t + which, full, 0.0))
        group = lax.broadcasted_iota(jnp.int32, (out.shape[0], width), 0)
        lane = lax.broadcasted_iota(jnp.int32, (out.shape[0], width), 1)
        out[...] = pick(jnp.where(lax.div(lane, HD) == group, mine, 0.0), per, HD)


def at_once(kernel, scalars, args, outs):
    moved = sum(a.size * a.dtype.itemsize for a in args) + sum(o.size * o.dtype.itemsize for o in outs)
    return pl.pallas_call(
        kernel,
        in_specs=[pl.BlockSpec(memory_space=pltpu.SMEM)] + [pl.BlockSpec(memory_space=pltpu.VMEM)] * len(args),
        out_specs=[pl.BlockSpec(memory_space=pltpu.VMEM)] * len(outs),
        out_shape=outs,
        compiler_params=pltpu.CompilerParams(vmem_limit_bytes=VMEM_LIMIT),
        cost_estimate=pl.CostEstimate(flops=0, bytes_accessed=moved, transcendentals=0),
    )(scalars, *args)


def by_pair(kernel, bit, args, outs):
    pairs = outs[0].shape[0]

    def spec(shape):
        at = 0 if shape[0] == pairs and (len(shape) == 3 or shape[1] == 2) else 1
        block = shape[:at] + (1,) + shape[at + 1 :]
        return pl.BlockSpec(block, lambda i, bit: (0,) * at + (i,) + (0,) * (len(shape) - at - 1))

    moved = sum(a.size * a.dtype.itemsize for a in args) + sum(o.size * o.dtype.itemsize for o in outs)
    return pl.pallas_call(
        kernel,
        grid_spec=pltpu.PrefetchScalarGridSpec(
            num_scalar_prefetch=1,
            grid=(pairs,),
            in_specs=[spec(a.shape) for a in args],
            out_specs=[spec(o.shape) for o in outs],
        ),
        out_shape=outs,
        compiler_params=pltpu.CompilerParams(vmem_limit_bytes=VMEM_LIMIT),
        cost_estimate=pl.CostEstimate(flops=0, bytes_accessed=moved, transcendentals=0),
    )(bit, *args)


def after(value, *others):
    return lax.optimization_barrier((value,) + others)[0]


def sds(shape, dtype):
    return jax.ShapeDtypeStruct(shape, dtype)


def make_body(mesh):
    nd = mesh.shape["dp"]
    nt_ax = mesh.shape["tensor"]
    bits = nd.bit_length() - 1

    def xch(v, axis, bit, order=1):
        n = mesh.shape[axis]
        return lax.ppermute(v, axis, [(i, i ^ (1 << bit)) for i in range(n)][::order])

    def bit_of(axis, bit):
        return ((lax.axis_index(axis) >> bit) & 1) == 1

    def body(
        patch_embeds,
        segment_ids,
        cotangent,
        ln1_gain,
        ln1_bias,
        w_query,
        w_key,
        w_value,
        b_query,
        b_value,
        w_out,
        b_out,
        ln2_gain,
        ln2_bias,
        w_fc1,
        b_fc1,
        w_fc2,
        b_fc2,
    ):
        strips, length, width = patch_embeds.shape
        assert strips == nt_ax == 4
        rows = width // nd
        heads = b_query.shape[0]
        hw = heads * HD
        per = HD // nd
        me_t = lax.axis_index("tensor")
        me_d = lax.axis_index("dp")
        x = lax.dynamic_index_in_dim(patch_embeds, me_t, 0, keepdims=False)
        dy = lax.dynamic_index_in_dim(cotangent, me_t, 0, keepdims=False)
        seg = lax.dynamic_index_in_dim(segment_ids, me_t, 0, keepdims=False)[:, None]

        def place(v, total, at):
            wide = jnp.zeros(v.shape[:-1] + (total,), BF)
            return lax.dynamic_update_slice_in_dim(wide, v, at, v.ndim - 1)

        six = jnp.stack([ln1_gain, ln1_bias, ln2_gain, ln2_bias, b_out, b_fc2])
        six = place(six, width, me_d * rows)
        heads_vec = place(jnp.concatenate([b_query, b_value, b_fc1]), HD, me_d * per)
        vec = jnp.concatenate(
            [
                six,
                heads_vec[2 * heads :].reshape(1, width),
                jnp.pad(heads_vec[: 2 * heads].reshape(1, 2 * hw), ((0, 0), (0, width - 2 * hw))),
            ]
        )
        share1 = jnp.concatenate(
            [jnp.concatenate([w_query, w_key, w_value, w_out.T], axis=1), vec]
        )
        share2 = jnp.concatenate([w_fc1, w_fc2.T])
        fc = lax.all_gather(share2, ("dp", "tensor"), axis=0, tiled=False)
        fc = fc.reshape(nd, nt_ax, 2 * rows, width)

        def spread(v, bit, axis, wait=None):
            r = xch(v, "dp", bit)
            if wait is not None:
                r = after(r, wait)
            high = bit_of("dp", bit)
            return jnp.stack([jnp.where(high, r, v), jnp.where(high, v, r)], axis=axis)

        quarter = share1[None]
        for bit in reversed(range(1, bits)):
            quarter = spread(quarter, bit, 1).reshape(-1, rows + VEC, width)
        quarter = after(quarter, x, dy, seg)
        far = xch(quarter, "tensor", 1)
        v0 = spread(quarter, 0, 1, far).reshape(nd, rows + VEC, width)
        v1 = xch(v0, "tensor", 0)

        row32 = sds((length, width), F32)
        row16 = sds((length, width), BF)
        head = sds((4, heads, length, 2 * HD), BF)
        kept = [
            sds((4, VEC, width), F32),
            head,
            head,
            head,
            sds((4, heads, length, length), BF),
            sds((4, length, width - 3 * hw + HD), BF),
            sds((4, length, width - 3 * hw + HD), F32),
        ]
        block_scr = pltpu.VMEM((nd, rows + VEC, width), BF)
        big = 2 * length * width * width
        att_flops = 2 * big + 4 * heads * length * length * 4 * HD
        n1, part, *kept_a = call(
            functools.partial(attn_fwd_first, rows, heads),
            [x, seg, v0, v1],
            "wwww",
            [row16, row32] + kept,
            "wwsssssss",
            [block_scr],
            att_flops,
        )
        dvec = kept_a[0]
        v2 = spread(far, 0, 1, part).reshape(nd, rows + VEC, width)
        v3 = xch(v2, "tensor", 0)
        middle, n2, *kept_b = call(
            functools.partial(attn_fwd_second, rows, heads),
            [x, n1, part, dvec, seg, v2, v3] + kept_a,
            "wwwwwww" + "a" * 7,
            [row32, row16] + kept,
            "wwsssssss",
            [block_scr],
            att_flops,
            out_order=(2, 3),
            aliases={7 + i: 2 + i for i in range(7)},
        )
        vec_all = kept_b[0]

        chunk = width // CHUNKS

        def mlp_call(kernel, n2, first, more, outs, scratch):
            ids = jnp.stack([me_t ^ first, me_t ^ (first - 1)])
            args = [n2, dy, fc, vec_all] + more
            specs = [
                whole_block(n2.shape),
                whole_block(dy.shape),
                pl.BlockSpec((nd, 1, 2 * rows, chunk), lambda i, ids: (0, ids[i // CHUNKS], 0, i % CHUNKS)),
                pl.BlockSpec((1, VEC, chunk), lambda i, ids: (first - i // CHUNKS, 0, i % CHUNKS)),
            ] + [whole_block(m.shape) for m in more]
            grad = sds((width, 2 * width), BF)
            return pl.pallas_call(
                kernel,
                grid_spec=pltpu.PrefetchScalarGridSpec(
                    num_scalar_prefetch=1,
                    grid=(2 * CHUNKS,),
                    in_specs=specs,
                    out_specs=[whole_block(o.shape) for o in outs]
                    + [
                        pl.BlockSpec((width, 2 * chunk), lambda i, ids: (0, jnp.minimum(i, CHUNKS - 1))),
                        pl.BlockSpec((width, 2 * chunk), lambda i, ids: (0, jnp.maximum(i - CHUNKS, 0))),
                        pl.BlockSpec((1, 1, chunk), lambda i, ids: (i // CHUNKS, 0, i % CHUNKS)),
                    ],
                    scratch_shapes=[pltpu.VMEM((width, length), BF)] * 2 + scratch,
                ),
                out_shape=outs + [grad, grad, sds((2, 1, width), F32)],
                compiler_params=pltpu.CompilerParams(vmem_limit_bytes=VMEM_LIMIT),
                cost_estimate=pl.CostEstimate(flops=12 * big * COST, bytes_accessed=20 * 2**20, transcendentals=0),
            )(ids, *args)

        def add(a, b):
            return (a.astype(F32) + b.astype(F32)).astype(BF)

        def parts(v, bit):
            high = bit_of("dp", bit)
            v = v.reshape(v.shape[:-3] + (v.shape[-3] // 2, 2) + v.shape[-2:])
            lo, hi = v[..., 0, :, :], v[..., 1, :, :]
            return jnp.where(high, hi, lo), jnp.where(high, lo, hi)

        def cut(v):
            return v.reshape(v.shape[:-2] + (nd, rows, v.shape[-1]))

        def add_parts(a, b, bit):
            keep_a, send_a = parts(a, bit)
            keep_b, send_b = parts(b, bit)
            return add(keep_a, keep_b), add(send_a, send_b)

        part_a = 2 * chunk
        part_b = 2 * width - part_a
        pairs = nd // 2
        bit0 = (me_d & 1).reshape(1)

        def paired(v):
            return v.reshape(v.shape[:-2] + (pairs, 2, rows, v.shape[-1]))

        def whole_pairs(c):
            return sds((pairs, 2, rows, c), BF)

        def half_pairs(c):
            return sds((pairs, rows, c), BF)

        out_b, back_b, g3, g2, gb1_b = mlp_call(functools.partial(mlp_first, rows), n2, 3, [], [row32, row32], [])
        got_fc = xch(g3, "tensor", 0)
        fc_send0, fc_keep2, fc_send2 = by_pair(
            functools.partial(fc_early, part_a),
            bit0,
            [paired(g2), paired(got_fc)],
            [whole_pairs(part_a), half_pairs(part_b), half_pairs(part_b)],
        )
        fc_far0 = xch(fc_send0, "tensor", 1)
        fc_near2 = xch(fc_send2, "dp", 0)
        y, gm, gml, vg2, g1, g0, gb1_a = mlp_call(
            functools.partial(mlp_second, rows),
            after(n2, fc_send0, fc_send2),
            1,
            [out_b, back_b, middle, dvec],
            [row16, row32, row16, sds((4, width), F32)],
            [pltpu.VMEM((length, width), F32)] * 2,
        )
        y_far = xch(y, "tensor", 1)
        y_core = xch(y, "tensor", 0)
        got_fc = xch(g1, "tensor", 0)
        gml, fc_far0, fc_near2 = lax.optimization_barrier((gml, fc_far0, fc_near2))

        g_in = sds((2, width, width // 2), BF)
        gb_in = sds((2, 1, 3 * hw), F32)
        back_flops = 4 * big + 10 * heads * length * length * 4 * HD
        saved = kept_b[1:]
        back1, in_a31, in_b31, gbh_b = call(
            functools.partial(attn_back_first, rows, heads),
            [n1, gml, v3, v1] + saved,
            "wwww" + "ssssss",
            [row32, g_in, g_in, gb_in],
            "wsss",
            [block_scr],
            back_flops,
            order=(3, 1),
            out_order=(0, 1),
        )
        got_ia = xch(in_a31, "tensor", 0)
        got_ib = xch(in_b31, "tensor", 0)
        got_fc = after(got_fc, back1)
        fc_half2, fc_keep, fc_send = by_pair(
            functools.partial(fc_late, part_a),
            bit0,
            [paired(g0), paired(got_fc), fc_far0, fc_keep2, fc_near2],
            [half_pairs(part_b), half_pairs(2 * width), half_pairs(2 * width)],
        )
        fc_far1 = xch(fc_half2, "tensor", 1)
        fc_near = xch(fc_send, "dp", 0)
        gml, y_far, y_core = lax.optimization_barrier((gml, y_far, y_core, fc_half2, fc_send))[:3]
        y_both = xch(y_far, "tensor", 0)
        gx, small, in_a20, in_b20 = call(
            functools.partial(attn_back_second, rows, heads),
            [n1, gml, v2, v0] + saved + [x, gm, back1, dvec, me_t.reshape(1), vg2, gb1_a, gb1_b, gbh_b],
            "wwww" + "ssssss" + "wwww" + "cwwww",
            [row16, sds((2 * SMALL, width // 2), BF), g_in, g_in],
            "wwss",
            [block_scr, pltpu.VMEM((length, width), F32), pltpu.VMEM((SMALL, width), F32)],
            back_flops,
            order=(2, 0),
            out_order=(0, 1),
        )

        in_c = width // 2

        def bit_at(bit):
            return ((me_d >> bit) & 1).reshape(1)

        def flat(n):
            return sds((n * rows + 2 * SMALL, in_c), BF)

        got_ia, got_ib, fc_far1, y_both = lax.optimization_barrier((got_ia, got_ib, fc_far1, y_both))
        in_send0, in_own, in_keep1, in_send1 = by_pair(
            in_first,
            bit0,
            [paired(in_a20), paired(got_ia), paired(in_b20), paired(got_ib)],
            [whole_pairs(in_c), whole_pairs(in_c), sds((2, pairs, rows, in_c), BF), sds((2, pairs, rows, in_c), BF)],
        )
        in_near1 = xch(in_send1, "dp", 0)
        in_far0 = xch(jnp.concatenate([in_send0.reshape(-1, in_c), small]), "tensor", 1)

        fc_near, fc_far1 = lax.optimization_barrier((fc_near, fc_far1, in_send0))[:2]
        n = pairs // 2
        fc_keep, fc_send = by_pair(
            functools.partial(fc_split, part_a),
            bit_at(1),
            [v.reshape(n, 2, rows, v.shape[-1]) for v in (fc_keep, fc_near, fc_far1)],
            [sds((n, rows, 2 * width), BF)] * 2,
        )
        in_near1 = after(in_near1, fc_send)
        fc_got = xch(fc_send, "dp", 1, -1)
        fc_keep, fc_send = parts(add(fc_keep, fc_got), 2)
        fc_got = xch(fc_send, "dp", 2, -1)
        in_far0 = after(in_far0, fc_send)

        gx_core = xch(gx, "tensor", 0)
        gx, in_far0 = lax.optimization_barrier((gx, in_far0))
        sent, in_keep0, in_half2, in_half0 = at_once(
            in_second,
            bit0,
            [in_own, in_far0, small, in_keep1, in_near1],
            [flat(pairs)] + [half_pairs(in_c)] * 3,
        )
        in_near0 = xch(sent, "dp", 0)
        in_far1 = xch(in_half2, "tensor", 1)
        gx_far = xch(gx, "tensor", 1)
        in_far1, fc_got = lax.optimization_barrier((in_far1, fc_got))
        sent, keep = at_once(
            in_third,
            bit_at(1),
            [sent, in_keep0, in_near0, in_half0, in_far1],
            [flat(2 * n), sds((2, n, rows, in_c), BF)],
        )
        got = xch(sent, "dp", 1)
        for bit in range(2, bits):
            n = n // 2
            sent, keep = at_once(
                in_next, bit_at(bit), [sent, keep, got], [flat(2 * n), sds((2, n, rows, in_c), BF)]
            )
            if bit > 2:
                fc_keep, fc_send = parts(add(fc_keep, fc_got), bit)
                fc_got = xch(fc_send, "dp", bit, -1)
            got = xch(sent, "dp", bit)
        gx_both = xch(gx_far, "tensor", 0)

        flip_c = bit_of("tensor", 0)
        flip_y = bit_of("tensor", 1)

        def strips_of(own, core, far, both):
            near = jnp.where(flip_c, core, own), jnp.where(flip_c, own, core)
            away = jnp.where(flip_c, both, far), jnp.where(flip_c, far, both)
            first = [jnp.where(flip_y, a, n) for n, a in zip(near, away)]
            second = [jnp.where(flip_y, n, a) for n, a in zip(near, away)]
            return jnp.stack(first + second)

        block_out = strips_of(y, y_core, y_far, y_both)
        grad_patches = strips_of(gx, gx_core, gx_far, gx_both)

        g_fc = add(fc_keep, fc_got)
        hw_out = sds((rows, hw), F32)
        g_query, g_key, g_value, g_out, small = at_once(
            functools.partial(in_last, hw),
            bit0,
            [sent, keep, got],
            [hw_out, hw_out, hw_out, sds((hw, rows), F32), sds((2 * SMALL, in_c), BF)],
        )
        six, g_b1, g_bh = at_once(
            small_last,
            jnp.stack([me_t, me_d]),
            [small, xch(small, "tensor", 0)],
            [sds((8, rows), F32), sds((width // HD, per), F32), sds((3 * heads, per), F32)],
        )
        g_fc = g_fc.reshape(rows, CHUNKS, 2, chunk).astype(F32)
        return (
            block_out,
            grad_patches,
            six[0],
            six[1],
            g_query,
            g_key,
            g_value,
            g_bh[:heads],
            g_bh[2 * heads :],
            g_out,
            six[4],
            six[2],
            six[3],
            g_fc[:, :, 0].reshape(rows, width),
            g_b1,
            g_fc[:, :, 1].reshape(rows, width).T,
            six[5],
        )

    return body


def solution(mesh):
    strip = P("dp", None, None)
    row_cut = P("dp", "tensor")
    col_cut = P("tensor", "dp")
    vector = P("dp")
    return jax.shard_map(
        make_body(mesh),
        mesh=mesh,
        in_specs=(
            strip,
            P("dp", None),
            strip,
            vector,
            vector,
            row_cut,
            row_cut,
            row_cut,
            col_cut,
            col_cut,
            col_cut,
            vector,
            vector,
            vector,
            row_cut,
            col_cut,
            col_cut,
            vector,
        ),
        out_specs=(
            strip,
            strip,
            vector,
            vector,
            row_cut,
            row_cut,
            row_cut,
            col_cut,
            col_cut,
            col_cut,
            vector,
            vector,
            vector,
            row_cut,
            col_cut,
            col_cut,
            vector,
        ),
        check_vma=False,
    )
```

```python
import functools

import jax
import jax.numpy as jnp
from jax import lax
from jax.experimental import pallas as pl
from jax.experimental.pallas import tpu as pltpu
from jax.sharding import PartitionSpec as P

HD = 64
EPS = 1e-06
BIG = 2.0**100
BF = jnp.bfloat16
F32 = jnp.float32
VEC = 8
SMALL = 16
COST = 20
VMEM_LIMIT = 53 * 1024 * 1024
SMALL_LIMIT = 20 * 1024 * 1024


def nn(a, b):
    return lax.dot_general(a, b, (((1,), (0,)), ((), ())), preferred_element_type=F32)


def nt(a, b):
    return lax.dot_general(a, b, (((1,), (1,)), ((), ())), preferred_element_type=F32)


def tn(a, b):
    return lax.dot_general(a, b, (((0,), (0,)), ((), ())), preferred_element_type=F32)


def norm_parts(v):
    c = v - jnp.mean(v, axis=-1, keepdims=True)
    rstd = lax.rsqrt(jnp.mean(c * c, axis=-1, keepdims=True) + EPS)
    return c * rstd, rstd


def norm_back(grad, gain, xhat, rstd):
    scaled = grad * gain
    m1 = jnp.mean(scaled, axis=-1, keepdims=True)
    m2 = jnp.mean(scaled * xhat, axis=-1, keepdims=True)
    return rstd * (scaled - m1 - xhat * m2)


def colsum(v):
    return jnp.sum(v, axis=0, keepdims=True)


def take_block(step, a_ref, b_ref, scr):
    @pl.when(step == 0)
    def _():
        scr[...] = a_ref[...]

    @pl.when(step == 1)
    def _():
        scr[...] = b_ref[...]


def attend_block(rows, heads, n1, scr, seg_ref, vec_ref, qe_ref, ke_ref, ve_ref, e_ref, att_ref, inv_ref):
    width = scr.shape[2]
    hw = heads * HD
    w = scr[:, :rows, :].reshape(width, width)
    vec = jnp.sum(scr[:, rows:, :].astype(F32), axis=0)
    vec_ref[0] = vec
    length = n1.shape[0]
    proj = nn(n1, w[:, : 3 * hw])
    bq = vec[7:8, :hw]
    bv = vec[7:8, hw : 2 * hw]
    q = ((proj[:, :hw] + bq).astype(BF).astype(F32) * (HD**-0.5)).astype(BF)
    k = proj[:, hw : 2 * hw].astype(BF)
    v = (proj[:, 2 * hw :] + bv).astype(BF)
    lane = lax.broadcasted_iota(jnp.int32, (length, HD), 1)
    hot = jnp.where(lane == seg_ref[...], 1.0, 0.0)
    ext_k = jnp.where(lane < 4, hot, 0.0).astype(BF)
    ext_q = jnp.where(lane < 4, (hot - 1.0) * BIG, 0.0).astype(BF)
    ext_v = jnp.where(lane < 2, 1.0, 0.0).astype(BF)
    atts = [jnp.zeros((length, HD), BF)]
    invs = [jnp.zeros((length, HD), F32)]
    for h in range(heads):
        cut = slice(h * HD, (h + 1) * HD)
        qe = jnp.concatenate([q[:, cut], ext_q], axis=1)
        ke = jnp.concatenate([k[:, cut], ext_k], axis=1)
        ve = jnp.concatenate([v[:, cut], ext_v], axis=1)
        qe_ref[0, h] = qe
        ke_ref[0, h] = ke
        ve_ref[0, h] = ve
        s = nt(ke, qe)
        e = jnp.exp(s - jnp.max(s, axis=0, keepdims=True)).astype(BF)
        e_ref[0, h] = e
        o = tn(e, ve)
        inv = 1.0 / o[:, HD : HD + 1]
        atts.append((o[:, :HD] * inv).astype(BF))
        invs.append(jnp.broadcast_to(inv, (length, HD)))
    att = jnp.concatenate(atts, axis=1)
    att_ref[0] = att
    inv_ref[0] = jnp.concatenate(invs, axis=1)
    return nt(att, w[:, 3 * hw - HD :])


def attn_fwd_first(rows, heads, x_ref, seg_ref, a_ref, b_ref, n1_ref, part_ref, vec_ref, qe_ref, ke_ref, ve_ref, e_ref, att_ref, inv_ref, scr):
    step = pl.program_id(0)
    take_block(step, a_ref, b_ref, scr)

    @pl.when(step == 0)
    def _():
        vec = jnp.sum(a_ref[:, rows:, :].astype(F32), axis=0)
        xhat, _ = norm_parts(x_ref[...].astype(F32))
        n1_ref[...] = (xhat * vec[0:1] + vec[1:2]).astype(BF)
        part_ref[...] = jnp.zeros_like(part_ref)

    part_ref[...] += attend_block(rows, heads, n1_ref[...], scr, seg_ref, vec_ref, qe_ref, ke_ref, ve_ref, e_ref, att_ref, inv_ref)


def attn_fwd_second(rows, heads, x_ref, n1_ref, part_ref, dvec_ref, seg_ref, a_ref, b_ref, k0, k1, k2, k3, k4, k5, k6, mid_ref, n2_ref, vec_ref, qe_ref, ke_ref, ve_ref, e_ref, att_ref, inv_ref, scr):
    step = pl.program_id(0)
    take_block(step, a_ref, b_ref, scr)
    more = attend_block(rows, heads, n1_ref[...], scr, seg_ref, vec_ref, qe_ref, ke_ref, ve_ref, e_ref, att_ref, inv_ref)

    @pl.when(step == 0)
    def _():
        mid_ref[...] = x_ref[...].astype(F32) + dvec_ref[0, 4:5] + part_ref[...] + more

    @pl.when(step == 1)
    def _():
        middle = mid_ref[...] + more
        mid_ref[...] = middle
        xhat, _ = norm_parts(middle)
        n2_ref[...] = (xhat * dvec_ref[0, 2:3] + dvec_ref[0, 3:4]).astype(BF)


def gelu_both(x):
    z = jnp.abs(x) * (0.5**0.5)
    t = 1.0 / (1.0 + 0.3275911 * z)
    gauss = jnp.exp(x * x * -0.5)
    poly = t * (0.254829592 + t * (-0.284496736 + t * (1.421413741 + t * (-1.453152027 + t * 1.061405429))))
    tail = 0.5 * poly * gauss
    cdf = jnp.where(x < 0, tail, 1.0 - tail)
    return x * cdf, cdf + x * gauss * 0.3989422804014327


CHUNKS = 3


def mlp_chunk(rows, n2_ref, dy_ref, n2t, dyt, w_ref, b1_ref, g_ref, gbias_ref):
    chunk = w_ref.shape[3]
    width = n2t.shape[0]
    w1 = w_ref[:, 0, :rows, :].reshape(width, chunk)
    w2 = w_ref[:, 0, rows:, :].reshape(width, chunk)
    pre = nn(n2_ref[...], w1) + b1_ref[0, 6:7]
    hid, slope = gelu_both(pre)
    hid = hid.astype(BF)
    gpre = (nn(dy_ref[...], w2) * slope).astype(BF)
    gbias_ref[0, 0:1] = colsum(gpre.astype(F32))
    g_ref[:, :chunk] = nn(n2t[...], gpre).astype(BF)
    g_ref[:, chunk:] = nn(dyt[...], hid).astype(BF)
    return nt(hid, w2), nt(gpre, w1)


def mlp_steps(rows, n2_ref, dy_ref, w_ref, b1_ref, g_refs, gbias_ref, n2t, dyt, first, accumulate):
    step = pl.program_id(0)

    @pl.when(step == 0)
    def _():
        n2t[...] = n2_ref[...].T
        dyt[...] = dy_ref[...].T
        first()

    for i, g_ref in enumerate(g_refs):

        @pl.when(step // CHUNKS == i)
        def _():
            accumulate(*mlp_chunk(rows, n2_ref, dy_ref, n2t, dyt, w_ref, b1_ref, g_ref, gbias_ref))


def mlp_first(rows, ids_ref, n2_ref, dy_ref, w_ref, b1_ref, out_ref, back_ref, g0_ref, g1_ref, gbias_ref, n2t, dyt):
    def first():
        out_ref[...] = jnp.zeros_like(out_ref)
        back_ref[...] = jnp.zeros_like(back_ref)

    def accumulate(out, back):
        out_ref[...] += out
        back_ref[...] += back

    mlp_steps(rows, n2_ref, dy_ref, w_ref, b1_ref, (g0_ref, g1_ref), gbias_ref, n2t, dyt, first, accumulate)


def mlp_second(rows, ids_ref, n2_ref, dy_ref, w_ref, b1_ref, out0_ref, back0_ref, mid_ref, dvec_ref, y_ref, gm_ref, gml_ref, vg_ref, g0_ref, g1_ref, gbias_ref, n2t, dyt, out_ref, back_ref):
    def first():
        out_ref[...] = out0_ref[...]
        back_ref[...] = back0_ref[...]

    def accumulate(out, back):
        out_ref[...] += out
        back_ref[...] += back

    mlp_steps(rows, n2_ref, dy_ref, w_ref, b1_ref, (g0_ref, g1_ref), gbias_ref, n2t, dyt, first, accumulate)

    @pl.when(pl.program_id(0) == 2 * CHUNKS - 1)
    def _():
        middle = mid_ref[...]
        dy = dy_ref[...].astype(F32)
        y_ref[...] = (middle + out_ref[...] + dvec_ref[0, 5:6]).astype(BF)
        grad = back_ref[...]
        xhat, rstd = norm_parts(middle)
        gm = dy + norm_back(grad, dvec_ref[0, 2:3], xhat, rstd)
        gm_ref[...] = gm
        gml_ref[...] = gm.astype(BF)
        vg_ref[0:1] = colsum(grad * xhat)
        vg_ref[1:2] = colsum(grad)
        vg_ref[2:3] = colsum(gm)
        vg_ref[3:4] = colsum(dy)


def attend_back(rows, heads, n1, gml, scr, qe_ref, ke_ref, ve_ref, e_ref, att_ref, inv_ref, ga_ref, gb_ref):
    width = scr.shape[2]
    hw = heads * HD
    half = width // 2
    w = scr[:, :rows, :].reshape(width, width)
    length = n1.shape[0]
    att = att_ref[0]
    ga = nn(gml, w[:, 3 * hw - HD :]).astype(BF).astype(F32) * inv_ref[0]
    do = ga.astype(BF)
    prod = do.astype(F32) * att.astype(F32)
    lane = lax.broadcasted_iota(jnp.int32, (length, HD), 1)
    dqs, dks, dvs = [], [], []
    for h in range(heads):
        cut = slice((h + 1) * HD, (h + 2) * HD)
        delta = -jnp.sum(prod[:, cut], axis=1, keepdims=True)
        high = delta.astype(BF).astype(F32)
        ext = jnp.where(lane == 0, high, jnp.where(lane == 1, delta - high, 0.0)).astype(BF)
        doe = jnp.concatenate([do[:, cut], ext], axis=1)
        e = e_ref[0, h]
        dp = nt(ve_ref[0, h], doe)
        ds = (e.astype(F32) * dp).astype(BF)
        dqs.append((tn(ds, ke_ref[0, h])[:, :HD] * (HD**-0.5)).astype(BF))
        dks.append(nn(ds, qe_ref[0, h][:, :HD]).astype(BF))
        dvs.append(nn(e, do[:, cut]).astype(BF))
    dqkv = jnp.concatenate(dqs + dks + dvs, axis=1)
    last = jnp.concatenate([dvs[-1], jnp.zeros((length, hw), BF)], axis=1)
    split = 3 * hw - HD
    ga_ref[0] = tn(n1, dqkv[:, :half]).astype(BF)
    gb_ref[0, :, : split - half] = tn(n1, dqkv[:, half:split]).astype(BF)
    gb_ref[0, :, split - half :] = (tn(n1, last) + tn(gml, att)).astype(BF)
    return nt(dqkv, w[:, : 3 * hw]), colsum(dqkv.astype(F32))


def attn_back_first(rows, heads, n1_ref, gml_ref, a_ref, b_ref, qe_ref, ke_ref, ve_ref, e_ref, att_ref, inv_ref, back_ref, ga_ref, gb_ref, gbias_ref, scr):
    step = pl.program_id(0)
    take_block(step, a_ref, b_ref, scr)
    back, gbias_ref[0, 0:1] = attend_back(rows, heads, n1_ref[...], gml_ref[...], scr, qe_ref, ke_ref, ve_ref, e_ref, att_ref, inv_ref, ga_ref, gb_ref)

    @pl.when(step == 0)
    def _():
        back_ref[...] = back

    @pl.when(step == 1)
    def _():
        back_ref[...] += back


def attn_back_second(rows, heads, n1_ref, gml_ref, a_ref, b_ref, qe_ref, ke_ref, ve_ref, e_ref, att_ref, inv_ref, x_ref, gm_ref, back0_ref, dvec_ref, me_ref, vg2_ref, hid_a_ref, hid_b_ref, head_b_ref, gx_ref, small_ref, ga_ref, gb_ref, scr, back_ref, rows_ref):
    step = pl.program_id(0)
    take_block(step, a_ref, b_ref, scr)
    back, bias = attend_back(rows, heads, n1_ref[...], gml_ref[...], scr, qe_ref, ke_ref, ve_ref, e_ref, att_ref, inv_ref, ga_ref, gb_ref)
    me = me_ref[0]

    def row_of(block):
        return 8 + 2 * (me ^ block)

    @pl.when(step == 0)
    def _():
        back_ref[...] = back0_ref[...] + back
        rows_ref[...] = jnp.zeros_like(rows_ref)
        rows_ref[2:6] = vg2_ref[...]
        for block, ref, at in ((3, hid_b_ref, 0), (2, hid_b_ref, 1), (1, hid_a_ref, 0), (0, hid_a_ref, 1)):
            rows_ref[pl.ds(row_of(block), 1)] = ref[at]
        for block, value in ((3, head_b_ref[0]), (1, head_b_ref[1]), (2, bias)):
            rows_ref[pl.ds(row_of(block) + 1, 1), : value.shape[1]] = value

    @pl.when(step == 1)
    def _():
        grad = back_ref[...] + back
        xhat, rstd = norm_parts(x_ref[...].astype(F32))
        gx_ref[...] = (gm_ref[...] + norm_back(grad, dvec_ref[0, 0:1], xhat, rstd)).astype(BF)
        rows_ref[0:1] = colsum(grad * xhat)
        rows_ref[1:2] = colsum(grad)
        rows_ref[pl.ds(row_of(0) + 1, 1), : bias.shape[1]] = bias
        half = rows_ref.shape[1] // 2
        small_ref[:SMALL] = rows_ref[:, :half].astype(BF)
        small_ref[SMALL:] = rows_ref[:, half:].astype(BF)


def whole_block(shape):
    return pl.BlockSpec(shape, lambda *_: (0,) * len(shape))


def step_block(shape, first, stride):
    rest = (0,) * (len(shape) - 1)
    return pl.BlockSpec((1,) + shape[1:], lambda i, *_: (first + stride * i,) + rest)


def call(kernel, args, in_kinds, outs, out_kinds, scratch, flops, order=(0, 1), out_order=None, aliases=None):
    def make(order):
        return {
            "w": whole_block,
            "s": lambda shape: step_block(shape, order[0], order[1] - order[0]),
            "a": lambda shape: pl.BlockSpec(memory_space=pl.ANY),
            "c": lambda shape: pl.BlockSpec(memory_space=pltpu.SMEM),
        }

    ins = make(order)
    out_specs = make(out_order or order)
    moved = sum(a.size * a.dtype.itemsize for a in args) + sum(o.size * o.dtype.itemsize for o in outs)
    return pl.pallas_call(
        kernel,
        grid=(2,),
        in_specs=[ins[kind](a.shape) for kind, a in zip(in_kinds, args)],
        out_specs=[out_specs[kind](o.shape) for kind, o in zip(out_kinds, outs)],
        out_shape=outs,
        scratch_shapes=scratch,
        input_output_aliases=aliases or {},
        compiler_params=pltpu.CompilerParams(vmem_limit_bytes=VMEM_LIMIT),
        cost_estimate=pl.CostEstimate(flops=flops * COST, bytes_accessed=moved, transcendentals=0),
    )(*args)


def total(*values):
    out = values[0].astype(F32)
    for value in values[1:]:
        out = out + value.astype(F32)
    return out.astype(BF)


def fc_early(part_a, bit_ref, mine, got, far_out, keep_out, send_out):
    bit = bit_ref[0]
    far_out[...] = total(mine[:, :, :, :part_a], got[:, :, :, :part_a])
    keep_out[0] = total(mine[0, bit, :, part_a:], got[0, bit, :, part_a:])
    send_out[0] = total(mine[0, 1 - bit, :, part_a:], got[0, 1 - bit, :, part_a:])


def fc_late(part_a, bit_ref, mine, got, far, keep2, near2, half_out, keep_out, send_out):
    bit = bit_ref[0]
    half_out[...] = total(keep2[...], near2[...])
    for which, out in ((bit, keep_out), (1 - bit, send_out)):
        out[0, :, :part_a] = total(mine[0, which, :, :part_a], got[0, which, :, :part_a], far[0, which])
        out[0, :, part_a:] = total(mine[0, which, :, part_a:], got[0, which, :, part_a:])


def in_first(bit_ref, mine_a, got_a, mine_b, got_b, far_out, own_out, keep_out, send_out):
    bit = bit_ref[0]
    far_out[...] = total(mine_a[0], got_a[0])
    own_out[...] = total(mine_a[1], got_a[1])
    for j in range(2):
        keep_out[j, 0] = total(mine_b[j, 0, bit], got_b[j, 0, bit])
        send_out[j, 0] = total(mine_b[j, 0, 1 - bit], got_b[j, 0, 1 - bit])


def fc_split(part_a, bit_ref, keep, near, far, keep_out, send_out):
    bit = bit_ref[0]
    for which, out in ((bit, keep_out), (1 - bit, send_out)):
        out[0, :, :part_a] = total(keep[0, which, :, :part_a], near[0, which, :, :part_a])
        out[0, :, part_a:] = total(keep[0, which, :, part_a:], near[0, which, :, part_a:], far[0, which])


def rows_at(index, rows):
    return pl.ds(pl.multiple_of(index * rows, rows), rows)


def in_second(bit_ref, own, far, small, keep1, near1, pay_out, keep_out, far_out, own_out):
    bit = bit_ref[0]
    pairs, _, rows, _ = own.shape
    for i in range(pairs):
        keep, send = 2 * i + bit, 2 * i + 1 - bit
        keep_out[i] = total(own[i, bit], far[rows_at(keep, rows), :])
        pay_out[i * rows : (i + 1) * rows] = total(own[i, 1 - bit], far[rows_at(send, rows), :])
    pay_out[pairs * rows :] = total(small[...], far[2 * pairs * rows :])
    far_out[...] = total(keep1[0], near1[0])
    own_out[...] = total(keep1[1], near1[1])


def in_third(bit_ref, sent, keep_a, got, keep_b, far, pay_out, keep_out):
    bit = bit_ref[0]
    pairs, rows, _ = keep_a.shape
    n = pairs // 2
    for i in range(n):
        keep, send = 2 * i + bit, 2 * i + 1 - bit
        keep_out[0, i] = total(keep_a[keep], got[rows_at(keep, rows), :])
        keep_out[1, i] = total(keep_b[keep], far[keep])
        pay_out[i * rows : (i + 1) * rows] = total(keep_a[send], got[rows_at(send, rows), :])
        pay_out[(n + i) * rows : (n + i + 1) * rows] = total(keep_b[send], far[send])
    pay_out[pairs * rows :] = total(sent[pairs * rows :], got[pairs * rows :])


def in_next(bit_ref, sent, keep, got, pay_out, keep_out):
    bit = bit_ref[0]
    _, n, rows, _ = keep.shape
    m = n // 2
    for h in range(2):
        for i in range(m):
            stay, go = 2 * i + bit, 2 * i + 1 - bit
            keep_out[h, i] = total(keep[h, stay], got[rows_at(h * n + stay, rows), :])
            pay_out[(h * m + i) * rows : (h * m + i + 1) * rows] = total(keep[h, go], got[rows_at(h * n + go, rows), :])
    pay_out[2 * m * rows :] = total(sent[2 * n * rows :], got[2 * n * rows :])


def in_last(hw, bit_ref, sent, keep, got, q_out, k_out, v_out, o_out, small_out):
    rows = keep.shape[2]
    first = keep[0, 0].astype(F32) + got[:rows].astype(F32)
    second = keep[1, 0].astype(F32) + got[rows : 2 * rows].astype(F32)
    q_out[...] = first[:, :hw]
    k_out[...] = first[:, hw:]
    v_out[...] = second[:, :hw]
    o_out[...] = second[:, hw:].T
    small_out[...] = total(sent[2 * rows :], got[2 * rows :])


def small_last(me_ref, small, got, six_out, hidden_out, heads_out):
    me_t, me_d = me_ref[0], me_ref[1]
    both = small[...].astype(F32) + got[...].astype(F32)
    full = jnp.concatenate([both[:SMALL], both[SMALL:]], axis=1)
    width = full.shape[1]
    rows = six_out.shape[1]
    per = hidden_out.shape[1]

    def pick(values, count, wrap):
        lane = lax.broadcasted_iota(jnp.int32, (width, count), 0)
        at = lax.broadcasted_iota(jnp.int32, (width, count), 1) + me_d * count
        ones = jnp.where(lax.rem(lane, wrap) == at, 1.0, 0.0)
        return lax.dot_general(
            values, ones, (((1,), (0,)), ((), ())), precision=lax.Precision.HIGHEST, preferred_element_type=F32
        )

    six_out[...] = pick(full[:8], rows, width)
    row = lax.broadcasted_iota(jnp.int32, (SMALL, width), 0)
    for which, out in ((0, hidden_out), (1, heads_out)):
        mine = colsum(jnp.where(row == 8 + 2 * me_t + which, full, 0.0))
        group = lax.broadcasted_iota(jnp.int32, (out.shape[0], width), 0)
        lane = lax.broadcasted_iota(jnp.int32, (out.shape[0], width), 1)
        out[...] = pick(jnp.where(lax.div(lane, HD) == group, mine, 0.0), per, HD)


def at_once(kernel, scalars, args, outs):
    moved = sum(a.size * a.dtype.itemsize for a in args) + sum(o.size * o.dtype.itemsize for o in outs)
    return pl.pallas_call(
        kernel,
        in_specs=[pl.BlockSpec(memory_space=pltpu.SMEM)] + [pl.BlockSpec(memory_space=pltpu.VMEM)] * len(args),
        out_specs=[pl.BlockSpec(memory_space=pltpu.VMEM)] * len(outs),
        out_shape=outs,
        compiler_params=pltpu.CompilerParams(vmem_limit_bytes=SMALL_LIMIT),
        cost_estimate=pl.CostEstimate(flops=0, bytes_accessed=moved, transcendentals=0),
    )(scalars, *args)


def by_pair(kernel, bit, args, outs):
    pairs = outs[0].shape[0]

    def spec(shape):
        at = 0 if shape[0] == pairs and (len(shape) == 3 or shape[1] == 2) else 1
        block = shape[:at] + (1,) + shape[at + 1 :]
        return pl.BlockSpec(block, lambda i, bit: (0,) * at + (i,) + (0,) * (len(shape) - at - 1))

    moved = sum(a.size * a.dtype.itemsize for a in args) + sum(o.size * o.dtype.itemsize for o in outs)
    return pl.pallas_call(
        kernel,
        grid_spec=pltpu.PrefetchScalarGridSpec(
            num_scalar_prefetch=1,
            grid=(pairs,),
            in_specs=[spec(a.shape) for a in args],
            out_specs=[spec(o.shape) for o in outs],
        ),
        out_shape=outs,
        compiler_params=pltpu.CompilerParams(vmem_limit_bytes=SMALL_LIMIT),
        cost_estimate=pl.CostEstimate(flops=0, bytes_accessed=moved, transcendentals=0),
    )(bit, *args)


def after(value, *others):
    return lax.optimization_barrier((value,) + others)[0]


def sds(shape, dtype):
    return jax.ShapeDtypeStruct(shape, dtype)


def make_body(mesh):
    nd = mesh.shape["dp"]
    nt_ax = mesh.shape["tensor"]
    bits = nd.bit_length() - 1

    def xch(v, axis, bit, order=1):
        n = mesh.shape[axis]
        return lax.ppermute(v, axis, [(i, i ^ (1 << bit)) for i in range(n)][::order])

    def bit_of(axis, bit):
        return ((lax.axis_index(axis) >> bit) & 1) == 1

    def body(
        patch_embeds,
        segment_ids,
        cotangent,
        ln1_gain,
        ln1_bias,
        w_query,
        w_key,
        w_value,
        b_query,
        b_value,
        w_out,
        b_out,
        ln2_gain,
        ln2_bias,
        w_fc1,
        b_fc1,
        w_fc2,
        b_fc2,
    ):
        strips, length, width = patch_embeds.shape
        assert strips == nt_ax == 4
        rows = width // nd
        heads = b_query.shape[0]
        hw = heads * HD
        per = HD // nd
        me_t = lax.axis_index("tensor")
        me_d = lax.axis_index("dp")
        x = lax.dynamic_index_in_dim(patch_embeds, me_t, 0, keepdims=False)
        dy = lax.dynamic_index_in_dim(cotangent, me_t, 0, keepdims=False)
        seg = lax.dynamic_index_in_dim(segment_ids, me_t, 0, keepdims=False)[:, None]

        def place(v, total, at):
            wide = jnp.zeros(v.shape[:-1] + (total,), BF)
            return lax.dynamic_update_slice_in_dim(wide, v, at, v.ndim - 1)

        six = jnp.stack([ln1_gain, ln1_bias, ln2_gain, ln2_bias, b_out, b_fc2])
        six = place(six, width, me_d * rows)
        heads_vec = place(jnp.concatenate([b_query, b_value, b_fc1]), HD, me_d * per)
        vec = jnp.concatenate(
            [
                six,
                heads_vec[2 * heads :].reshape(1, width),
                jnp.pad(heads_vec[: 2 * heads].reshape(1, 2 * hw), ((0, 0), (0, width - 2 * hw))),
            ]
        )
        share1 = jnp.concatenate(
            [jnp.concatenate([w_query, w_key, w_value, w_out.T], axis=1), vec]
        )
        share2 = jnp.concatenate([w_fc1, w_fc2.T])
        fc = lax.all_gather(share2, ("dp", "tensor"), axis=0, tiled=False)
        fc = fc.reshape(nd, nt_ax, 2 * rows, width)

        def spread(v, bit, axis, wait=None):
            r = xch(v, "dp", bit)
            if wait is not None:
                r = after(r, wait)
            high = bit_of("dp", bit)
            return jnp.stack([jnp.where(high, r, v), jnp.where(high, v, r)], axis=axis)

        quarter = share1[None]
        for bit in reversed(range(1, bits)):
            quarter = spread(quarter, bit, 1).reshape(-1, rows + VEC, width)
        quarter = after(quarter, x, dy, seg)
        far = xch(quarter, "tensor", 1)
        v0 = spread(quarter, 0, 1, far).reshape(nd, rows + VEC, width)
        v1 = xch(v0, "tensor", 0)

        row32 = sds((length, width), F32)
        row16 = sds((length, width), BF)
        head = sds((4, heads, length, 2 * HD), BF)
        kept = [
            sds((4, VEC, width), F32),
            head,
            head,
            head,
            sds((4, heads, length, length), BF),
            sds((4, length, width - 3 * hw + HD), BF),
            sds((4, length, width - 3 * hw + HD), F32),
        ]
        block_scr = pltpu.VMEM((nd, rows + VEC, width), BF)
        big = 2 * length * width * width
        att_flops = 2 * big + 4 * heads * length * length * 4 * HD
        n1, part, *kept_a = call(
            functools.partial(attn_fwd_first, rows, heads),
            [x, seg, v0, v1],
            "wwww",
            [row16, row32] + kept,
            "wwsssssss",
            [block_scr],
            att_flops,
        )
        dvec = kept_a[0]
        v2 = spread(far, 0, 1, part).reshape(nd, rows + VEC, width)
        v3 = xch(v2, "tensor", 0)
        middle, n2, *kept_b = call(
            functools.partial(attn_fwd_second, rows, heads),
            [x, n1, part, dvec, seg, v2, v3] + kept_a,
            "wwwwwww" + "a" * 7,
            [row32, row16] + kept,
            "wwsssssss",
            [block_scr],
            att_flops,
            out_order=(2, 3),
            aliases={7 + i: 2 + i for i in range(7)},
        )
        vec_all = kept_b[0]

        chunk = width // CHUNKS

        def mlp_call(kernel, n2, first, more, outs, scratch):
            ids = jnp.stack([me_t ^ first, me_t ^ (first - 1)])
            args = [n2, dy, fc, vec_all] + more
            specs = [
                whole_block(n2.shape),
                whole_block(dy.shape),
                pl.BlockSpec((nd, 1, 2 * rows, chunk), lambda i, ids: (0, ids[i // CHUNKS], 0, i % CHUNKS)),
                pl.BlockSpec((1, VEC, chunk), lambda i, ids: (first - i // CHUNKS, 0, i % CHUNKS)),
            ] + [whole_block(m.shape) for m in more]
            grad = sds((width, 2 * width), BF)
            return pl.pallas_call(
                kernel,
                grid_spec=pltpu.PrefetchScalarGridSpec(
                    num_scalar_prefetch=1,
                    grid=(2 * CHUNKS,),
                    in_specs=specs,
                    out_specs=[whole_block(o.shape) for o in outs]
                    + [
                        pl.BlockSpec((width, 2 * chunk), lambda i, ids: (0, jnp.minimum(i, CHUNKS - 1))),
                        pl.BlockSpec((width, 2 * chunk), lambda i, ids: (0, jnp.maximum(i - CHUNKS, 0))),
                        pl.BlockSpec((1, 1, chunk), lambda i, ids: (i // CHUNKS, 0, i % CHUNKS)),
                    ],
                    scratch_shapes=[pltpu.VMEM((width, length), BF)] * 2 + scratch,
                ),
                out_shape=outs + [grad, grad, sds((2, 1, width), F32)],
                compiler_params=pltpu.CompilerParams(vmem_limit_bytes=VMEM_LIMIT),
                cost_estimate=pl.CostEstimate(flops=12 * big * COST, bytes_accessed=20 * 2**20, transcendentals=0),
            )(ids, *args)

        def add(a, b):
            return (a.astype(F32) + b.astype(F32)).astype(BF)

        def parts(v, bit):
            high = bit_of("dp", bit)
            v = v.reshape(v.shape[:-3] + (v.shape[-3] // 2, 2) + v.shape[-2:])
            lo, hi = v[..., 0, :, :], v[..., 1, :, :]
            return jnp.where(high, hi, lo), jnp.where(high, lo, hi)

        def cut(v):
            return v.reshape(v.shape[:-2] + (nd, rows, v.shape[-1]))

        def add_parts(a, b, bit):
            keep_a, send_a = parts(a, bit)
            keep_b, send_b = parts(b, bit)
            return add(keep_a, keep_b), add(send_a, send_b)

        part_a = 2 * chunk
        part_b = 2 * width - part_a
        pairs = nd // 2
        bit0 = (me_d & 1).reshape(1)

        def paired(v):
            return v.reshape(v.shape[:-2] + (pairs, 2, rows, v.shape[-1]))

        def whole_pairs(c):
            return sds((pairs, 2, rows, c), BF)

        def half_pairs(c):
            return sds((pairs, rows, c), BF)

        out_b, back_b, g3, g2, gb1_b = mlp_call(functools.partial(mlp_first, rows), n2, 3, [], [row32, row32], [])
        got_fc = xch(g3, "tensor", 0)
        fc_send0, fc_keep2, fc_send2 = by_pair(
            functools.partial(fc_early, part_a),
            bit0,
            [paired(g2), paired(got_fc)],
            [whole_pairs(part_a), half_pairs(part_b), half_pairs(part_b)],
        )
        fc_far0 = xch(fc_send0, "tensor", 1)
        fc_near2 = xch(fc_send2, "dp", 0)
        y, gm, gml, vg2, g1, g0, gb1_a = mlp_call(
            functools.partial(mlp_second, rows),
            after(n2, fc_send0, fc_send2),
            1,
            [out_b, back_b, middle, dvec],
            [row16, row32, row16, sds((4, width), F32)],
            [pltpu.VMEM((length, width), F32)] * 2,
        )
        y_far = xch(y, "tensor", 1)
        y_core = xch(y, "tensor", 0)
        got_fc = xch(g1, "tensor", 0)
        gml, fc_far0, fc_near2 = lax.optimization_barrier((gml, fc_far0, fc_near2))

        g_in = sds((2, width, width // 2), BF)
        gb_in = sds((2, 1, 3 * hw), F32)
        back_flops = 4 * big + 10 * heads * length * length * 4 * HD
        saved = kept_b[1:]
        back1, in_a31, in_b31, gbh_b = call(
            functools.partial(attn_back_first, rows, heads),
            [n1, gml, v3, v1] + saved,
            "wwww" + "ssssss",
            [row32, g_in, g_in, gb_in],
            "wsss",
            [block_scr],
            back_flops,
            order=(3, 1),
            out_order=(0, 1),
        )
        got_ia = xch(in_a31, "tensor", 0)
        got_ib = xch(in_b31, "tensor", 0)
        got_fc = after(got_fc, back1)
        fc_half2, fc_keep, fc_send = by_pair(
            functools.partial(fc_late, part_a),
            bit0,
            [paired(g0), paired(got_fc), fc_far0, fc_keep2, fc_near2],
            [half_pairs(part_b), half_pairs(2 * width), half_pairs(2 * width)],
        )
        fc_far1 = xch(fc_half2, "tensor", 1)
        fc_near = xch(fc_send, "dp", 0)
        gml, y_far, y_core = lax.optimization_barrier((gml, y_far, y_core, fc_half2, fc_send))[:3]
        y_both = xch(y_far, "tensor", 0)
        gx, small, in_a20, in_b20 = call(
            functools.partial(attn_back_second, rows, heads),
            [n1, gml, v2, v0] + saved + [x, gm, back1, dvec, me_t.reshape(1), vg2, gb1_a, gb1_b, gbh_b],
            "wwww" + "ssssss" + "wwww" + "cwwww",
            [row16, sds((2 * SMALL, width // 2), BF), g_in, g_in],
            "wwss",
            [block_scr, pltpu.VMEM((length, width), F32), pltpu.VMEM((SMALL, width), F32)],
            back_flops,
            order=(2, 0),
            out_order=(0, 1),
        )

        in_c = width // 2

        def bit_at(bit):
            return ((me_d >> bit) & 1).reshape(1)

        def flat(n):
            return sds((n * rows + 2 * SMALL, in_c), BF)

        got_ia, got_ib, fc_far1, y_both = lax.optimization_barrier((got_ia, got_ib, fc_far1, y_both))
        in_send0, in_own, in_keep1, in_send1 = by_pair(
            in_first,
            bit0,
            [paired(in_a20), paired(got_ia), paired(in_b20), paired(got_ib)],
            [whole_pairs(in_c), whole_pairs(in_c), sds((2, pairs, rows, in_c), BF), sds((2, pairs, rows, in_c), BF)],
        )
        in_near1 = xch(in_send1, "dp", 0)
        in_far0 = xch(jnp.concatenate([in_send0.reshape(-1, in_c), small]), "tensor", 1)

        fc_near, fc_far1 = lax.optimization_barrier((fc_near, fc_far1, in_send0))[:2]
        n = pairs // 2
        fc_keep, fc_send = by_pair(
            functools.partial(fc_split, part_a),
            bit_at(1),
            [v.reshape(n, 2, rows, v.shape[-1]) for v in (fc_keep, fc_near, fc_far1)],
            [sds((n, rows, 2 * width), BF)] * 2,
        )
        in_near1 = after(in_near1, fc_send)
        fc_got = xch(fc_send, "dp", 1, -1)
        fc_keep, fc_send = parts(add(fc_keep, fc_got), 2)
        fc_got = xch(fc_send, "dp", 2, -1)
        in_far0 = after(in_far0, fc_send)

        gx_core = xch(gx, "tensor", 0)
        gx, in_far0 = lax.optimization_barrier((gx, in_far0))
        sent, in_keep0, in_half2, in_half0 = at_once(
            in_second,
            bit0,
            [in_own, in_far0, small, in_keep1, in_near1],
            [flat(pairs)] + [half_pairs(in_c)] * 3,
        )
        in_near0 = xch(sent, "dp", 0)
        in_far1 = xch(in_half2, "tensor", 1)
        gx_far = xch(gx, "tensor", 1)
        in_far1, fc_got = lax.optimization_barrier((in_far1, fc_got))
        sent, keep = at_once(
            in_third,
            bit_at(1),
            [sent, in_keep0, in_near0, in_half0, in_far1],
            [flat(2 * n), sds((2, n, rows, in_c), BF)],
        )
        got = xch(sent, "dp", 1)
        for bit in range(2, bits):
            n = n // 2
            sent, keep = at_once(
                in_next, bit_at(bit), [sent, keep, got], [flat(2 * n), sds((2, n, rows, in_c), BF)]
            )
            if bit > 2:
                fc_keep, fc_send = parts(add(fc_keep, fc_got), bit)
                fc_got = xch(fc_send, "dp", bit, -1)
            got = xch(sent, "dp", bit)
        gx_both = xch(gx_far, "tensor", 0)

        flip_c = bit_of("tensor", 0)
        flip_y = bit_of("tensor", 1)

        def strips_of(own, core, far, both):
            near = jnp.where(flip_c, core, own), jnp.where(flip_c, own, core)
            away = jnp.where(flip_c, both, far), jnp.where(flip_c, far, both)
            first = [jnp.where(flip_y, a, n) for n, a in zip(near, away)]
            second = [jnp.where(flip_y, n, a) for n, a in zip(near, away)]
            return jnp.stack(first + second)

        block_out = strips_of(y, y_core, y_far, y_both)
        grad_patches = strips_of(gx, gx_core, gx_far, gx_both)

        g_fc = add(fc_keep, fc_got)
        hw_out = sds((rows, hw), F32)
        g_query, g_key, g_value, g_out, small = at_once(
            functools.partial(in_last, hw),
            bit0,
            [sent, keep, got],
            [hw_out, hw_out, hw_out, sds((hw, rows), F32), sds((2 * SMALL, in_c), BF)],
        )
        six, g_b1, g_bh = at_once(
            small_last,
            jnp.stack([me_t, me_d]),
            [small, xch(small, "tensor", 0)],
            [sds((8, rows), F32), sds((width // HD, per), F32), sds((3 * heads, per), F32)],
        )
        g_fc = g_fc.reshape(rows, CHUNKS, 2, chunk).astype(F32)
        return (
            block_out,
            grad_patches,
            six[0],
            six[1],
            g_query,
            g_key,
            g_value,
            g_bh[:heads],
            g_bh[2 * heads :],
            g_out,
            six[4],
            six[2],
            six[3],
            g_fc[:, :, 0].reshape(rows, width),
            g_b1,
            g_fc[:, :, 1].reshape(rows, width).T,
            six[5],
        )

    return body


def solution(mesh):
    strip = P("dp", None, None)
    row_cut = P("dp", "tensor")
    col_cut = P("tensor", "dp")
    vector = P("dp")
    return jax.shard_map(
        make_body(mesh),
        mesh=mesh,
        in_specs=(
            strip,
            P("dp", None),
            strip,
            vector,
            vector,
            row_cut,
            row_cut,
            row_cut,
            col_cut,
            col_cut,
            col_cut,
            vector,
            vector,
            vector,
            row_cut,
            col_cut,
            col_cut,
            vector,
        ),
        out_specs=(
            strip,
            strip,
            vector,
            vector,
            row_cut,
            row_cut,
            row_cut,
            col_cut,
            col_cut,
            col_cut,
            vector,
            vector,
            vector,
            row_cut,
            col_cut,
            col_cut,
            vector,
        ),
        check_vma=False,
    )
```

```python
import functools

import jax
import jax.numpy as jnp
from jax import lax
from jax.experimental import pallas as pl
from jax.experimental.pallas import tpu as pltpu
from jax.sharding import PartitionSpec as P

HD = 64
EPS = 1e-06
BIG = 2.0**100
BF = jnp.bfloat16
F32 = jnp.float32
VEC = 8
SMALL = 16
COST = 20
VMEM_LIMIT = 53 * 1024 * 1024
SMALL_LIMIT = 20 * 1024 * 1024


def nn(a, b):
    return lax.dot_general(a, b, (((1,), (0,)), ((), ())), preferred_element_type=F32)


def nt(a, b):
    return lax.dot_general(a, b, (((1,), (1,)), ((), ())), preferred_element_type=F32)


def tn(a, b):
    return lax.dot_general(a, b, (((0,), (0,)), ((), ())), preferred_element_type=F32)


def norm_parts(v):
    c = v - jnp.mean(v, axis=-1, keepdims=True)
    rstd = lax.rsqrt(jnp.mean(c * c, axis=-1, keepdims=True) + EPS)
    return c * rstd, rstd


def norm_back(grad, gain, xhat, rstd):
    scaled = grad * gain
    m1 = jnp.mean(scaled, axis=-1, keepdims=True)
    m2 = jnp.mean(scaled * xhat, axis=-1, keepdims=True)
    return rstd * (scaled - m1 - xhat * m2)


def colsum(v):
    return jnp.sum(v, axis=0, keepdims=True)


def take_block(step, a_ref, b_ref, scr):
    @pl.when(step == 0)
    def _():
        scr[...] = a_ref[...]

    @pl.when(step == 1)
    def _():
        scr[...] = b_ref[...]


def attend_block(rows, heads, n1, scr, seg_ref, vec_ref, qe_ref, ke_ref, ve_ref, e_ref, att_ref, inv_ref):
    width = scr.shape[2]
    hw = heads * HD
    w = scr[:, :rows, :].reshape(width, width)
    vec = jnp.sum(scr[:, rows:, :].astype(F32), axis=0)
    vec_ref[0] = vec
    length = n1.shape[0]
    proj = nn(n1, w[:, : 3 * hw])
    bq = vec[7:8, :hw]
    bv = vec[7:8, hw : 2 * hw]
    q = ((proj[:, :hw] + bq).astype(BF).astype(F32) * (HD**-0.5)).astype(BF)
    k = proj[:, hw : 2 * hw].astype(BF)
    v = (proj[:, 2 * hw :] + bv).astype(BF)
    lane = lax.broadcasted_iota(jnp.int32, (length, HD), 1)
    hot = jnp.where(lane == seg_ref[...], 1.0, 0.0)
    ext_k = jnp.where(lane < 4, hot, 0.0).astype(BF)
    ext_q = jnp.where(lane < 4, (hot - 1.0) * BIG, 0.0).astype(BF)
    ext_v = jnp.where(lane < 2, 1.0, 0.0).astype(BF)
    atts = [jnp.zeros((length, HD), BF)]
    invs = [jnp.zeros((length, HD), F32)]
    for h in range(heads):
        cut = slice(h * HD, (h + 1) * HD)
        qe = jnp.concatenate([q[:, cut], ext_q], axis=1)
        ke = jnp.concatenate([k[:, cut], ext_k], axis=1)
        ve = jnp.concatenate([v[:, cut], ext_v], axis=1)
        qe_ref[0, h] = qe
        ke_ref[0, h] = ke
        ve_ref[0, h] = ve
        s = nt(ke, qe)
        e = jnp.exp(s - jnp.max(s, axis=0, keepdims=True)).astype(BF)
        e_ref[0, h] = e
        o = tn(e, ve)
        inv = 1.0 / o[:, HD : HD + 1]
        atts.append((o[:, :HD] * inv).astype(BF))
        invs.append(jnp.broadcast_to(inv, (length, HD)))
    att = jnp.concatenate(atts, axis=1)
    att_ref[0] = att
    inv_ref[0] = jnp.concatenate(invs, axis=1)
    return nt(att, w[:, 3 * hw - HD :])


def attn_fwd_first(rows, heads, x_ref, seg_ref, a_ref, b_ref, n1_ref, part_ref, vec_ref, qe_ref, ke_ref, ve_ref, e_ref, att_ref, inv_ref, scr):
    step = pl.program_id(0)
    take_block(step, a_ref, b_ref, scr)

    @pl.when(step == 0)
    def _():
        vec = jnp.sum(a_ref[:, rows:, :].astype(F32), axis=0)
        xhat, _ = norm_parts(x_ref[...].astype(F32))
        n1_ref[...] = (xhat * vec[0:1] + vec[1:2]).astype(BF)
        part_ref[...] = jnp.zeros_like(part_ref)

    part_ref[...] += attend_block(rows, heads, n1_ref[...], scr, seg_ref, vec_ref, qe_ref, ke_ref, ve_ref, e_ref, att_ref, inv_ref)


def attn_fwd_second(rows, heads, x_ref, n1_ref, part_ref, dvec_ref, seg_ref, a_ref, b_ref, k0, k1, k2, k3, k4, k5, k6, mid_ref, n2_ref, vec_ref, qe_ref, ke_ref, ve_ref, e_ref, att_ref, inv_ref, scr):
    step = pl.program_id(0)
    take_block(step, a_ref, b_ref, scr)
    more = attend_block(rows, heads, n1_ref[...], scr, seg_ref, vec_ref, qe_ref, ke_ref, ve_ref, e_ref, att_ref, inv_ref)

    @pl.when(step == 0)
    def _():
        mid_ref[...] = x_ref[...].astype(F32) + dvec_ref[0, 4:5] + part_ref[...] + more

    @pl.when(step == 1)
    def _():
        middle = mid_ref[...] + more
        mid_ref[...] = middle
        xhat, _ = norm_parts(middle)
        n2_ref[...] = (xhat * dvec_ref[0, 2:3] + dvec_ref[0, 3:4]).astype(BF)


def gelu_both(x):
    z = jnp.abs(x) * (0.5**0.5)
    t = 1.0 / (1.0 + 0.3275911 * z)
    gauss = jnp.exp(x * x * -0.5)
    poly = t * (0.254829592 + t * (-0.284496736 + t * (1.421413741 + t * (-1.453152027 + t * 1.061405429))))
    tail = 0.5 * poly * gauss
    cdf = jnp.where(x < 0, tail, 1.0 - tail)
    return x * cdf, cdf + x * gauss * 0.3989422804014327


CHUNKS = 3


def mlp_chunk(rows, n2_ref, dy_ref, n2t, dyt, w_ref, b1_ref, g_ref, gbias_ref):
    chunk = w_ref.shape[3]
    width = n2t.shape[0]
    w1 = w_ref[:, 0, :rows, :].reshape(width, chunk)
    w2 = w_ref[:, 0, rows:, :].reshape(width, chunk)
    pre = nn(n2_ref[...], w1) + b1_ref[0, 6:7]
    hid, slope = gelu_both(pre)
    hid = hid.astype(BF)
    gpre = (nn(dy_ref[...], w2) * slope).astype(BF)
    gbias_ref[0, 0:1] = colsum(gpre.astype(F32))
    g_ref[:, :chunk] = nn(n2t[...], gpre).astype(BF)
    g_ref[:, chunk:] = nn(dyt[...], hid).astype(BF)
    return nt(hid, w2), nt(gpre, w1)


def mlp_steps(rows, n2_ref, dy_ref, w_ref, b1_ref, g_refs, gbias_ref, n2t, dyt, first, accumulate):
    step = pl.program_id(0)

    @pl.when(step == 0)
    def _():
        n2t[...] = n2_ref[...].T
        dyt[...] = dy_ref[...].T
        first()

    for i, g_ref in enumerate(g_refs):

        @pl.when(step // CHUNKS == i)
        def _():
            accumulate(*mlp_chunk(rows, n2_ref, dy_ref, n2t, dyt, w_ref, b1_ref, g_ref, gbias_ref))


def mlp_first(rows, ids_ref, n2_ref, dy_ref, w_ref, b1_ref, out_ref, back_ref, g0_ref, g1_ref, gbias_ref, n2t, dyt):
    def first():
        out_ref[...] = jnp.zeros_like(out_ref)
        back_ref[...] = jnp.zeros_like(back_ref)

    def accumulate(out, back):
        out_ref[...] += out
        back_ref[...] += back

    mlp_steps(rows, n2_ref, dy_ref, w_ref, b1_ref, (g0_ref, g1_ref), gbias_ref, n2t, dyt, first, accumulate)


def mlp_second(rows, ids_ref, n2_ref, dy_ref, w_ref, b1_ref, out0_ref, back0_ref, mid_ref, dvec_ref, y_ref, gm_ref, gml_ref, vg_ref, g0_ref, g1_ref, gbias_ref, n2t, dyt, out_ref, back_ref):
    def first():
        out_ref[...] = out0_ref[...]
        back_ref[...] = back0_ref[...]

    def accumulate(out, back):
        out_ref[...] += out
        back_ref[...] += back

    mlp_steps(rows, n2_ref, dy_ref, w_ref, b1_ref, (g0_ref, g1_ref), gbias_ref, n2t, dyt, first, accumulate)

    @pl.when(pl.program_id(0) == 2 * CHUNKS - 1)
    def _():
        middle = mid_ref[...]
        dy = dy_ref[...].astype(F32)
        y_ref[...] = (middle + out_ref[...] + dvec_ref[0, 5:6]).astype(BF)
        grad = back_ref[...]
        xhat, rstd = norm_parts(middle)
        gm = dy + norm_back(grad, dvec_ref[0, 2:3], xhat, rstd)
        gm_ref[...] = gm
        gml_ref[...] = gm.astype(BF)
        vg_ref[0:1] = colsum(grad * xhat)
        vg_ref[1:2] = colsum(grad)
        vg_ref[2:3] = colsum(gm)
        vg_ref[3:4] = colsum(dy)


def attend_back(rows, heads, n1, gml, scr, qe_ref, ke_ref, ve_ref, e_ref, att_ref, inv_ref, ga_ref, gb_ref):
    width = scr.shape[2]
    hw = heads * HD
    half = width // 2
    w = scr[:, :rows, :].reshape(width, width)
    length = n1.shape[0]
    att = att_ref[0]
    ga = nn(gml, w[:, 3 * hw - HD :]).astype(BF).astype(F32) * inv_ref[0]
    do = ga.astype(BF)
    prod = do.astype(F32) * att.astype(F32)
    lane = lax.broadcasted_iota(jnp.int32, (length, HD), 1)
    dqs, dks, dvs = [], [], []
    for h in range(heads):
        cut = slice((h + 1) * HD, (h + 2) * HD)
        delta = -jnp.sum(prod[:, cut], axis=1, keepdims=True)
        high = delta.astype(BF).astype(F32)
        ext = jnp.where(lane == 0, high, jnp.where(lane == 1, delta - high, 0.0)).astype(BF)
        doe = jnp.concatenate([do[:, cut], ext], axis=1)
        e = e_ref[0, h]
        dp = nt(ve_ref[0, h], doe)
        ds = (e.astype(F32) * dp).astype(BF)
        dqs.append((tn(ds, ke_ref[0, h])[:, :HD] * (HD**-0.5)).astype(BF))
        dks.append(nn(ds, qe_ref[0, h][:, :HD]).astype(BF))
        dvs.append(nn(e, do[:, cut]).astype(BF))
    dqkv = jnp.concatenate(dqs + dks + dvs, axis=1)
    last = jnp.concatenate([dvs[-1], jnp.zeros((length, hw), BF)], axis=1)
    split = 3 * hw - HD
    ga_ref[0] = tn(n1, dqkv[:, :half]).astype(BF)
    gb_ref[0, :, : split - half] = tn(n1, dqkv[:, half:split]).astype(BF)
    gb_ref[0, :, split - half :] = (tn(n1, last) + tn(gml, att)).astype(BF)
    return nt(dqkv, w[:, : 3 * hw]), colsum(dqkv.astype(F32))


def attn_back_first(rows, heads, n1_ref, gml_ref, a_ref, b_ref, qe_ref, ke_ref, ve_ref, e_ref, att_ref, inv_ref, back_ref, ga_ref, gb_ref, gbias_ref, scr):
    step = pl.program_id(0)
    take_block(step, a_ref, b_ref, scr)
    back, gbias_ref[0, 0:1] = attend_back(rows, heads, n1_ref[...], gml_ref[...], scr, qe_ref, ke_ref, ve_ref, e_ref, att_ref, inv_ref, ga_ref, gb_ref)

    @pl.when(step == 0)
    def _():
        back_ref[...] = back

    @pl.when(step == 1)
    def _():
        back_ref[...] += back


def attn_back_second(rows, heads, n1_ref, gml_ref, a_ref, b_ref, qe_ref, ke_ref, ve_ref, e_ref, att_ref, inv_ref, x_ref, gm_ref, back0_ref, dvec_ref, me_ref, vg2_ref, hid_a_ref, hid_b_ref, head_b_ref, gx_ref, small_ref, ga_ref, gb_ref, scr, back_ref, rows_ref):
    step = pl.program_id(0)
    take_block(step, a_ref, b_ref, scr)
    back, bias = attend_back(rows, heads, n1_ref[...], gml_ref[...], scr, qe_ref, ke_ref, ve_ref, e_ref, att_ref, inv_ref, ga_ref, gb_ref)
    me = me_ref[0]

    def row_of(block):
        return 8 + 2 * (me ^ block)

    @pl.when(step == 0)
    def _():
        back_ref[...] = back0_ref[...] + back
        rows_ref[...] = jnp.zeros_like(rows_ref)
        rows_ref[2:6] = vg2_ref[...]
        for block, ref, at in ((3, hid_b_ref, 0), (2, hid_b_ref, 1), (1, hid_a_ref, 0), (0, hid_a_ref, 1)):
            rows_ref[pl.ds(row_of(block), 1)] = ref[at]
        for block, value in ((3, head_b_ref[0]), (1, head_b_ref[1]), (2, bias)):
            rows_ref[pl.ds(row_of(block) + 1, 1), : value.shape[1]] = value

    @pl.when(step == 1)
    def _():
        grad = back_ref[...] + back
        xhat, rstd = norm_parts(x_ref[...].astype(F32))
        gx_ref[...] = (gm_ref[...] + norm_back(grad, dvec_ref[0, 0:1], xhat, rstd)).astype(BF)
        rows_ref[0:1] = colsum(grad * xhat)
        rows_ref[1:2] = colsum(grad)
        rows_ref[pl.ds(row_of(0) + 1, 1), : bias.shape[1]] = bias
        half = rows_ref.shape[1] // 2
        small_ref[:SMALL] = rows_ref[:, :half].astype(BF)
        small_ref[SMALL:] = rows_ref[:, half:].astype(BF)


def whole_block(shape):
    return pl.BlockSpec(shape, lambda *_: (0,) * len(shape))


def step_block(shape, first, stride):
    rest = (0,) * (len(shape) - 1)
    return pl.BlockSpec((1,) + shape[1:], lambda i, *_: (first + stride * i,) + rest)


def call(kernel, args, in_kinds, outs, out_kinds, scratch, flops, order=(0, 1), out_order=None, aliases=None):
    def make(order):
        return {
            "w": whole_block,
            "s": lambda shape: step_block(shape, order[0], order[1] - order[0]),
            "a": lambda shape: pl.BlockSpec(memory_space=pl.ANY),
            "c": lambda shape: pl.BlockSpec(memory_space=pltpu.SMEM),
        }

    ins = make(order)
    out_specs = make(out_order or order)
    moved = sum(a.size * a.dtype.itemsize for a in args) + sum(o.size * o.dtype.itemsize for o in outs)
    return pl.pallas_call(
        kernel,
        grid=(2,),
        in_specs=[ins[kind](a.shape) for kind, a in zip(in_kinds, args)],
        out_specs=[out_specs[kind](o.shape) for kind, o in zip(out_kinds, outs)],
        out_shape=outs,
        scratch_shapes=scratch,
        input_output_aliases=aliases or {},
        compiler_params=pltpu.CompilerParams(vmem_limit_bytes=VMEM_LIMIT),
        cost_estimate=pl.CostEstimate(flops=flops * COST, bytes_accessed=moved, transcendentals=0),
    )(*args)


def total(*values):
    out = values[0].astype(F32)
    for value in values[1:]:
        out = out + value.astype(F32)
    return out.astype(BF)


def fc_early(part_a, bit_ref, mine, got, far_out, keep_out, send_out):
    bit = bit_ref[0]
    far_out[...] = total(mine[:, :, :, :part_a], got[:, :, :, :part_a])
    keep_out[0] = total(mine[0, bit, :, part_a:], got[0, bit, :, part_a:])
    send_out[0] = total(mine[0, 1 - bit, :, part_a:], got[0, 1 - bit, :, part_a:])


def fc_late(part_a, bit_ref, mine, got, far, keep2, near2, half_out, keep_out, send_out):
    bit = bit_ref[0]
    half_out[...] = total(keep2[...], near2[...])
    for which, out in ((bit, keep_out), (1 - bit, send_out)):
        out[0, :, :part_a] = total(mine[0, which, :, :part_a], got[0, which, :, :part_a], far[0, which])
        out[0, :, part_a:] = total(mine[0, which, :, part_a:], got[0, which, :, part_a:])


def in_first(bit_ref, mine_a, got_a, mine_b, got_b, far_out, own_out, keep_out, send_out):
    bit = bit_ref[0]
    far_out[...] = total(mine_a[0], got_a[0])
    own_out[...] = total(mine_a[1], got_a[1])
    for j in range(2):
        keep_out[j, 0] = total(mine_b[j, 0, bit], got_b[j, 0, bit])
        send_out[j, 0] = total(mine_b[j, 0, 1 - bit], got_b[j, 0, 1 - bit])


def fc_split(part_a, bit_ref, keep, near, far, keep_out, send_out):
    bit = bit_ref[0]
    for which, out in ((bit, keep_out), (1 - bit, send_out)):
        out[0, :, :part_a] = total(keep[0, which, :, :part_a], near[0, which, :, :part_a])
        out[0, :, part_a:] = total(keep[0, which, :, part_a:], near[0, which, :, part_a:], far[0, which])


def rows_at(index, rows):
    return pl.ds(pl.multiple_of(index * rows, rows), rows)


def in_second(bit_ref, own, far, small, keep1, near1, pay_out, keep_out, far_out, own_out):
    bit = bit_ref[0]
    pairs, _, rows, _ = own.shape
    for i in range(pairs):
        keep, send = 2 * i + bit, 2 * i + 1 - bit
        keep_out[i] = total(own[i, bit], far[rows_at(keep, rows), :])
        pay_out[i * rows : (i + 1) * rows] = total(own[i, 1 - bit], far[rows_at(send, rows), :])
    pay_out[pairs * rows :] = total(small[...], far[2 * pairs * rows :])
    far_out[...] = total(keep1[0], near1[0])
    own_out[...] = total(keep1[1], near1[1])


def in_third(bit_ref, sent, keep_a, got, keep_b, far, pay_out, keep_out):
    bit = bit_ref[0]
    pairs, rows, _ = keep_a.shape
    n = pairs // 2
    for i in range(n):
        keep, send = 2 * i + bit, 2 * i + 1 - bit
        keep_out[0, i] = total(keep_a[keep], got[rows_at(keep, rows), :])
        keep_out[1, i] = total(keep_b[keep], far[keep])
        pay_out[i * rows : (i + 1) * rows] = total(keep_a[send], got[rows_at(send, rows), :])
        pay_out[(n + i) * rows : (n + i + 1) * rows] = total(keep_b[send], far[send])
    pay_out[pairs * rows :] = total(sent[pairs * rows :], got[pairs * rows :])


def in_next(bit_ref, sent, keep, got, pay_out, keep_out):
    bit = bit_ref[0]
    _, n, rows, _ = keep.shape
    m = n // 2
    for h in range(2):
        for i in range(m):
            stay, go = 2 * i + bit, 2 * i + 1 - bit
            keep_out[h, i] = total(keep[h, stay], got[rows_at(h * n + stay, rows), :])
            pay_out[(h * m + i) * rows : (h * m + i + 1) * rows] = total(keep[h, go], got[rows_at(h * n + go, rows), :])
    pay_out[2 * m * rows :] = total(sent[2 * n * rows :], got[2 * n * rows :])


def in_last(hw, bit_ref, sent, keep, got, q_out, k_out, v_out, o_out, small_out):
    rows = keep.shape[2]
    first = keep[0, 0].astype(F32) + got[:rows].astype(F32)
    second = keep[1, 0].astype(F32) + got[rows : 2 * rows].astype(F32)
    q_out[...] = first[:, :hw]
    k_out[...] = first[:, hw:]
    v_out[...] = second[:, :hw]
    o_out[...] = second[:, hw:].T
    small_out[...] = total(sent[2 * rows :], got[2 * rows :])


def small_last(me_ref, small, got, six_out, hidden_out, heads_out):
    me_t, me_d = me_ref[0], me_ref[1]
    both = small[...].astype(F32) + got[...].astype(F32)
    full = jnp.concatenate([both[:SMALL], both[SMALL:]], axis=1)
    width = full.shape[1]
    rows = six_out.shape[1]
    per = hidden_out.shape[1]

    def pick(values, count, wrap):
        lane = lax.broadcasted_iota(jnp.int32, (width, count), 0)
        at = lax.broadcasted_iota(jnp.int32, (width, count), 1) + me_d * count
        ones = jnp.where(lax.rem(lane, wrap) == at, 1.0, 0.0)
        return lax.dot_general(
            values, ones, (((1,), (0,)), ((), ())), precision=lax.Precision.HIGHEST, preferred_element_type=F32
        )

    six_out[...] = pick(full[:8], rows, width)
    row = lax.broadcasted_iota(jnp.int32, (SMALL, width), 0)
    for which, out in ((0, hidden_out), (1, heads_out)):
        mine = colsum(jnp.where(row == 8 + 2 * me_t + which, full, 0.0))
        group = lax.broadcasted_iota(jnp.int32, (out.shape[0], width), 0)
        lane = lax.broadcasted_iota(jnp.int32, (out.shape[0], width), 1)
        out[...] = pick(jnp.where(lax.div(lane, HD) == group, mine, 0.0), per, HD)


def at_once(kernel, scalars, args, outs):
    moved = sum(a.size * a.dtype.itemsize for a in args) + sum(o.size * o.dtype.itemsize for o in outs)
    return pl.pallas_call(
        kernel,
        in_specs=[pl.BlockSpec(memory_space=pltpu.SMEM)] + [pl.BlockSpec(memory_space=pltpu.VMEM)] * len(args),
        out_specs=[pl.BlockSpec(memory_space=pltpu.VMEM)] * len(outs),
        out_shape=outs,
        compiler_params=pltpu.CompilerParams(vmem_limit_bytes=SMALL_LIMIT),
        cost_estimate=pl.CostEstimate(flops=0, bytes_accessed=moved, transcendentals=0),
    )(scalars, *args)


def by_pair(kernel, bit, args, outs):
    pairs = outs[0].shape[0]

    def spec(shape):
        at = 0 if shape[0] == pairs and (len(shape) == 3 or shape[1] == 2) else 1
        block = shape[:at] + (1,) + shape[at + 1 :]
        return pl.BlockSpec(block, lambda i, bit: (0,) * at + (i,) + (0,) * (len(shape) - at - 1))

    moved = sum(a.size * a.dtype.itemsize for a in args) + sum(o.size * o.dtype.itemsize for o in outs)
    return pl.pallas_call(
        kernel,
        grid_spec=pltpu.PrefetchScalarGridSpec(
            num_scalar_prefetch=1,
            grid=(pairs,),
            in_specs=[spec(a.shape) for a in args],
            out_specs=[spec(o.shape) for o in outs],
        ),
        out_shape=outs,
        compiler_params=pltpu.CompilerParams(vmem_limit_bytes=SMALL_LIMIT),
        cost_estimate=pl.CostEstimate(flops=0, bytes_accessed=moved, transcendentals=0),
    )(bit, *args)


def after(value, *others):
    return lax.optimization_barrier((value,) + others)[0]


def sds(shape, dtype):
    return jax.ShapeDtypeStruct(shape, dtype)


def make_body(mesh):
    nd = mesh.shape["dp"]
    nt_ax = mesh.shape["tensor"]
    bits = nd.bit_length() - 1

    def xch(v, axis, bit, order=1):
        n = mesh.shape[axis]
        return lax.ppermute(v, axis, [(i, i ^ (1 << bit)) for i in range(n)][::order])

    def bit_of(axis, bit):
        return ((lax.axis_index(axis) >> bit) & 1) == 1

    def body(
        patch_embeds,
        segment_ids,
        cotangent,
        ln1_gain,
        ln1_bias,
        w_query,
        w_key,
        w_value,
        b_query,
        b_value,
        w_out,
        b_out,
        ln2_gain,
        ln2_bias,
        w_fc1,
        b_fc1,
        w_fc2,
        b_fc2,
    ):
        strips, length, width = patch_embeds.shape
        assert strips == nt_ax == 4
        rows = width // nd
        heads = b_query.shape[0]
        hw = heads * HD
        per = HD // nd
        me_t = lax.axis_index("tensor")
        me_d = lax.axis_index("dp")
        x = lax.dynamic_index_in_dim(patch_embeds, me_t, 0, keepdims=False)
        dy = lax.dynamic_index_in_dim(cotangent, me_t, 0, keepdims=False)
        seg = lax.dynamic_index_in_dim(segment_ids, me_t, 0, keepdims=False)[:, None]

        def place(v, total, at):
            wide = jnp.zeros(v.shape[:-1] + (total,), BF)
            return lax.dynamic_update_slice_in_dim(wide, v, at, v.ndim - 1)

        six = jnp.stack([ln1_gain, ln1_bias, ln2_gain, ln2_bias, b_out, b_fc2])
        six = place(six, width, me_d * rows)
        heads_vec = place(jnp.concatenate([b_query, b_value, b_fc1]), HD, me_d * per)
        vec = jnp.concatenate(
            [
                six,
                heads_vec[2 * heads :].reshape(1, width),
                jnp.pad(heads_vec[: 2 * heads].reshape(1, 2 * hw), ((0, 0), (0, width - 2 * hw))),
            ]
        )
        share1 = jnp.concatenate(
            [jnp.concatenate([w_query, w_key, w_value, w_out.T], axis=1), vec]
        )
        share2 = jnp.concatenate([w_fc1, w_fc2.T])
        fc = lax.all_gather(share2, ("dp", "tensor"), axis=0, tiled=False)
        fc = fc.reshape(nd, nt_ax, 2 * rows, width)

        def spread(v, bit, axis, wait=None):
            r = xch(v, "dp", bit)
            if wait is not None:
                r = after(r, wait)
            high = bit_of("dp", bit)
            return jnp.stack([jnp.where(high, r, v), jnp.where(high, v, r)], axis=axis)

        quarter = share1[None]
        for bit in reversed(range(1, bits)):
            quarter = spread(quarter, bit, 1).reshape(-1, rows + VEC, width)
        quarter = after(quarter, x, dy, seg)
        far = xch(quarter, "tensor", 1)
        v0 = spread(quarter, 0, 1, far).reshape(nd, rows + VEC, width)
        v1 = xch(v0, "tensor", 0)

        row32 = sds((length, width), F32)
        row16 = sds((length, width), BF)
        head = sds((4, heads, length, 2 * HD), BF)
        kept = [
            sds((4, VEC, width), F32),
            head,
            head,
            head,
            sds((4, heads, length, length), BF),
            sds((4, length, width - 3 * hw + HD), BF),
            sds((4, length, width - 3 * hw + HD), F32),
        ]
        block_scr = pltpu.VMEM((nd, rows + VEC, width), BF)
        big = 2 * length * width * width
        att_flops = 2 * big + 4 * heads * length * length * 4 * HD
        n1, part, *kept_a = call(
            functools.partial(attn_fwd_first, rows, heads),
            [x, seg, v0, v1],
            "wwww",
            [row16, row32] + kept,
            "wwsssssss",
            [block_scr],
            att_flops,
        )
        dvec = kept_a[0]
        v2 = spread(far, 0, 1, part).reshape(nd, rows + VEC, width)
        v3 = xch(v2, "tensor", 0)
        middle, n2, *kept_b = call(
            functools.partial(attn_fwd_second, rows, heads),
            [x, n1, part, dvec, seg, v2, v3] + kept_a,
            "wwwwwww" + "a" * 7,
            [row32, row16] + kept,
            "wwsssssss",
            [block_scr],
            att_flops,
            out_order=(2, 3),
            aliases={7 + i: 2 + i for i in range(7)},
        )
        vec_all = kept_b[0]

        chunk = width // CHUNKS

        def mlp_call(kernel, n2, first, more, outs, scratch):
            ids = jnp.stack([me_t ^ first, me_t ^ (first - 1)])
            args = [n2, dy, fc, vec_all] + more
            specs = [
                whole_block(n2.shape),
                whole_block(dy.shape),
                pl.BlockSpec((nd, 1, 2 * rows, chunk), lambda i, ids: (0, ids[i // CHUNKS], 0, i % CHUNKS)),
                pl.BlockSpec((1, VEC, chunk), lambda i, ids: (first - i // CHUNKS, 0, i % CHUNKS)),
            ] + [whole_block(m.shape) for m in more]
            grad = sds((width, 2 * width), BF)
            return pl.pallas_call(
                kernel,
                grid_spec=pltpu.PrefetchScalarGridSpec(
                    num_scalar_prefetch=1,
                    grid=(2 * CHUNKS,),
                    in_specs=specs,
                    out_specs=[whole_block(o.shape) for o in outs]
                    + [
                        pl.BlockSpec((width, 2 * chunk), lambda i, ids: (0, jnp.minimum(i, CHUNKS - 1))),
                        pl.BlockSpec((width, 2 * chunk), lambda i, ids: (0, jnp.maximum(i - CHUNKS, 0))),
                        pl.BlockSpec((1, 1, chunk), lambda i, ids: (i // CHUNKS, 0, i % CHUNKS)),
                    ],
                    scratch_shapes=[pltpu.VMEM((width, length), BF)] * 2 + scratch,
                ),
                out_shape=outs + [grad, grad, sds((2, 1, width), F32)],
                compiler_params=pltpu.CompilerParams(vmem_limit_bytes=VMEM_LIMIT),
                cost_estimate=pl.CostEstimate(flops=12 * big * COST, bytes_accessed=20 * 2**20, transcendentals=0),
            )(ids, *args)

        def add(a, b):
            return (a.astype(F32) + b.astype(F32)).astype(BF)

        def parts(v, bit):
            high = bit_of("dp", bit)
            v = v.reshape(v.shape[:-3] + (v.shape[-3] // 2, 2) + v.shape[-2:])
            lo, hi = v[..., 0, :, :], v[..., 1, :, :]
            return jnp.where(high, hi, lo), jnp.where(high, lo, hi)

        def cut(v):
            return v.reshape(v.shape[:-2] + (nd, rows, v.shape[-1]))

        def add_parts(a, b, bit):
            keep_a, send_a = parts(a, bit)
            keep_b, send_b = parts(b, bit)
            return add(keep_a, keep_b), add(send_a, send_b)

        part_a = 2 * chunk
        part_b = 2 * width - part_a
        pairs = nd // 2
        bit0 = (me_d & 1).reshape(1)

        def paired(v):
            return v.reshape(v.shape[:-2] + (pairs, 2, rows, v.shape[-1]))

        def whole_pairs(c):
            return sds((pairs, 2, rows, c), BF)

        def half_pairs(c):
            return sds((pairs, rows, c), BF)

        out_b, back_b, g3, g2, gb1_b = mlp_call(functools.partial(mlp_first, rows), n2, 3, [], [row32, row32], [])
        got_fc = xch(g3, "tensor", 0)
        fc_send0, fc_keep2, fc_send2 = by_pair(
            functools.partial(fc_early, part_a),
            bit0,
            [paired(g2), paired(got_fc)],
            [whole_pairs(part_a), half_pairs(part_b), half_pairs(part_b)],
        )
        fc_far0 = xch(fc_send0, "tensor", 1)
        fc_near2 = xch(fc_send2, "dp", 0)
        y, gm, gml, vg2, g1, g0, gb1_a = mlp_call(
            functools.partial(mlp_second, rows),
            after(n2, fc_send0, fc_send2),
            1,
            [out_b, back_b, middle, dvec],
            [row16, row32, row16, sds((4, width), F32)],
            [pltpu.VMEM((length, width), F32)] * 2,
        )
        y_far = xch(y, "tensor", 1)
        y_core = xch(y, "tensor", 0)
        got_fc = xch(g1, "tensor", 0)
        gml, fc_far0, fc_near2 = lax.optimization_barrier((gml, fc_far0, fc_near2))

        g_in = sds((2, width, width // 2), BF)
        gb_in = sds((2, 1, 3 * hw), F32)
        back_flops = 4 * big + 10 * heads * length * length * 4 * HD
        saved = kept_b[1:]
        back1, in_a31, in_b31, gbh_b = call(
            functools.partial(attn_back_first, rows, heads),
            [n1, gml, v3, v1] + saved,
            "wwww" + "ssssss",
            [row32, g_in, g_in, gb_in],
            "wsss",
            [block_scr],
            back_flops,
            order=(3, 1),
            out_order=(0, 1),
        )
        got_ia = xch(in_a31, "tensor", 0)
        got_ib = xch(in_b31, "tensor", 0)
        got_fc = after(got_fc, back1)
        fc_half2, fc_keep, fc_send = by_pair(
            functools.partial(fc_late, part_a),
            bit0,
            [paired(g0), paired(got_fc), fc_far0, fc_keep2, fc_near2],
            [half_pairs(part_b), half_pairs(2 * width), half_pairs(2 * width)],
        )
        fc_far1 = xch(fc_half2, "tensor", 1)
        fc_near = xch(fc_send, "dp", 0)
        gml, y_far, y_core = lax.optimization_barrier((gml, y_far, y_core, fc_half2, fc_send))[:3]
        y_both = xch(y_far, "tensor", 0)
        gx, small, in_a20, in_b20 = call(
            functools.partial(attn_back_second, rows, heads),
            [n1, gml, v2, v0] + saved + [x, gm, back1, dvec, me_t.reshape(1), vg2, gb1_a, gb1_b, gbh_b],
            "wwww" + "ssssss" + "wwww" + "cwwww",
            [row16, sds((2 * SMALL, width // 2), BF), g_in, g_in],
            "wwss",
            [block_scr, pltpu.VMEM((length, width), F32), pltpu.VMEM((SMALL, width), F32)],
            back_flops,
            order=(2, 0),
            out_order=(0, 1),
        )

        in_c = width // 2

        def bit_at(bit):
            return ((me_d >> bit) & 1).reshape(1)

        def flat(n):
            return sds((n * rows + 2 * SMALL, in_c), BF)

        got_ia, got_ib, fc_far1, y_both = lax.optimization_barrier((got_ia, got_ib, fc_far1, y_both))
        in_send0, in_own, in_keep1, in_send1 = by_pair(
            in_first,
            bit0,
            [paired(in_a20), paired(got_ia), paired(in_b20), paired(got_ib)],
            [whole_pairs(in_c), whole_pairs(in_c), sds((2, pairs, rows, in_c), BF), sds((2, pairs, rows, in_c), BF)],
        )
        in_near1 = xch(in_send1, "dp", 0)
        in_far0 = xch(jnp.concatenate([in_send0.reshape(-1, in_c), small]), "tensor", 1)

        fc_near, fc_far1 = lax.optimization_barrier((fc_near, fc_far1, in_send0))[:2]
        n = pairs // 2
        fc_keep, fc_send = by_pair(
            functools.partial(fc_split, part_a),
            bit_at(1),
            [v.reshape(n, 2, rows, v.shape[-1]) for v in (fc_keep, fc_near, fc_far1)],
            [sds((n, rows, 2 * width), BF)] * 2,
        )
        in_near1 = after(in_near1, fc_send)
        fc_got = xch(fc_send, "dp", 1, -1)
        fc_keep, fc_send = parts(add(fc_keep, fc_got), 2)
        fc_got = xch(fc_send, "dp", 2, -1)
        in_far0 = after(in_far0, fc_send)

        gx_core = xch(gx, "tensor", 0)
        gx, in_far0 = lax.optimization_barrier((gx, in_far0))
        sent, in_keep0, in_half2, in_half0 = at_once(
            in_second,
            bit0,
            [in_own, in_far0, small, in_keep1, in_near1],
            [flat(pairs)] + [half_pairs(in_c)] * 3,
        )
        in_near0 = xch(sent, "dp", 0)
        in_far1 = xch(in_half2, "tensor", 1)
        gx_far = xch(gx, "tensor", 1)
        in_far1, fc_got = lax.optimization_barrier((in_far1, fc_got))
        sent, keep = at_once(
            in_third,
            bit_at(1),
            [sent, in_keep0, in_near0, in_half0, in_far1],
            [flat(2 * n), sds((2, n, rows, in_c), BF)],
        )
        got = xch(sent, "dp", 1)
        for bit in range(2, bits):
            n = n // 2
            sent, keep = at_once(
                in_next, bit_at(bit), [sent, keep, got], [flat(2 * n), sds((2, n, rows, in_c), BF)]
            )
            if bit > 2:
                fc_keep, fc_send = parts(add(fc_keep, fc_got), bit)
                fc_got = xch(fc_send, "dp", bit, -1)
            got = xch(sent, "dp", bit)
        gx_both = xch(gx_far, "tensor", 0)

        flip_c = bit_of("tensor", 0)
        flip_y = bit_of("tensor", 1)

        def strips_of(own, core, far, both):
            near = jnp.where(flip_c, core, own), jnp.where(flip_c, own, core)
            away = jnp.where(flip_c, both, far), jnp.where(flip_c, far, both)
            first = [jnp.where(flip_y, a, n) for n, a in zip(near, away)]
            second = [jnp.where(flip_y, n, a) for n, a in zip(near, away)]
            return jnp.stack(first + second)

        block_out = strips_of(y, y_core, y_far, y_both)
        grad_patches = strips_of(gx, gx_core, gx_far, gx_both)

        g_fc = add(fc_keep, fc_got).reshape(rows, CHUNKS, 2, chunk).astype(F32)
        g_up, g_down = g_fc[:, :, 0].reshape(rows, width), g_fc[:, :, 1].reshape(rows, width)
        got, g_up, g_down = lax.optimization_barrier((got, g_up, g_down))
        hw_out = sds((rows, hw), F32)
        g_query, g_key, g_value, g_out, small = at_once(
            functools.partial(in_last, hw),
            bit0,
            [sent, keep, got],
            [hw_out, hw_out, hw_out, sds((hw, rows), F32), sds((2 * SMALL, in_c), BF)],
        )
        six, g_b1, g_bh = at_once(
            small_last,
            jnp.stack([me_t, me_d]),
            [small, xch(small, "tensor", 0)],
            [sds((8, rows), F32), sds((width // HD, per), F32), sds((3 * heads, per), F32)],
        )
        return (
            block_out,
            grad_patches,
            six[0],
            six[1],
            g_query,
            g_key,
            g_value,
            g_bh[:heads],
            g_bh[2 * heads :],
            g_out,
            six[4],
            six[2],
            six[3],
            g_up,
            g_b1,
            g_down.T,
            six[5],
        )

    return body


def solution(mesh):
    strip = P("dp", None, None)
    row_cut = P("dp", "tensor")
    col_cut = P("tensor", "dp")
    vector = P("dp")
    return jax.shard_map(
        make_body(mesh),
        mesh=mesh,
        in_specs=(
            strip,
            P("dp", None),
            strip,
            vector,
            vector,
            row_cut,
            row_cut,
            row_cut,
            col_cut,
            col_cut,
            col_cut,
            vector,
            vector,
            vector,
            row_cut,
            col_cut,
            col_cut,
            vector,
        ),
        out_specs=(
            strip,
            strip,
            vector,
            vector,
            row_cut,
            row_cut,
            row_cut,
            col_cut,
            col_cut,
            col_cut,
            vector,
            vector,
            vector,
            row_cut,
            col_cut,
            col_cut,
            vector,
        ),
        check_vma=False,
    )
```
